256 devices in a mesh: gz: 16 (over y_lo, z), gx: 4 (over y_hi, core), gy: 4 (over x).
Axes of the slice: x: 4, y: 4 (y_hi: 2, y_lo: 2; y = y_hi * 2 + y_lo), z: 8, core: 2. Of those that a mesh axis runs over, the one named last changes fastest.
Arguments:
- sections: bfloat16 [16, 2560, 2560], P('gz', 'gy', 'gx'), may hold values from -440 to 440
- peaks: int32 [16, 2, 40, 40], P('gz', None, 'gy', 'gx'), may hold values from 0 to 127
- valid: int32 [16, 40, 40], P('gz', 'gy', 'gx'), may hold values 0 or 1
Outputs:
- fit: float32 [16, 6, 40, 40], P('gz', None, 'gy', 'gx')
The draws below stay inside these ranges and needn't reach their ends.
All inputs are finite; a program needn't handle non-finite values. Where the reference program divides by a largest or mean magnitude, that divisor is 1e-20 or more. No bound on the sum of `valid` on one device may be relied on, other than what follows from the above.
Results may differ from the reference program's by a relative error of at most 0.0089.
Values may be sent and summed in bfloat16 or wider, within the bound.
A program may use at most 64 MiB of HBM per device.

```python
import math
import jax
import jax.numpy as jnp
from jax import lax

PATCH = 128
STRIDE = 64
WIN = 5
NSEC = 16
NY = 2560
NX = 2560
NPY = 40
NPX = 40


def draw_sections(key, part):
    first, second, third = jax.random.split(jax.random.fold_in(key, 11), 3)
    shape = (NSEC, NY, NX)
    base = jnp.clip(jax.random.normal(first, shape, jnp.float32), -4.0, 4.0)
    row_scale = jnp.exp(jax.random.uniform(second, (NSEC, NY, 1), jnp.float32, 0.0, math.log(10.0)))
    col_scale = jnp.exp(jax.random.uniform(third, (NSEC, 1, NX), jnp.float32, 0.0, math.log(10.0)))
    return (base * row_scale * col_scale).astype(jnp.bfloat16)


def place_ends(entries, stream_key, smallest, high):
    longest = entries.shape.index(max(entries.shape))
    spots = []
    for shift in (0, 1):
        where = [jax.random.randint(jax.random.fold_in(stream_key, axis), (), 0, length) for axis, length in enumerate(entries.shape)]
        where[longest] = (where[longest] + shift) % entries.shape[longest]
        spots.append(tuple(where))
    return entries.at[spots[0]].set(smallest).at[spots[1]].set(high)


def setup_inputs(seed: int = 0) -> dict:
    arg_keys = jax.random.split(jax.random.key(seed), 4)
    return {
        "sections": draw_sections(jax.random.fold_in(arg_keys[3], 71), 0),
        "peaks": place_ends(jax.random.randint(arg_keys[1], (NSEC, 2, NPY, NPX), 0, PATCH), jax.random.fold_in(arg_keys[1], 1), 0, PATCH - 1).astype(jnp.int32),
        "valid": place_ends((jax.random.randint(arg_keys[2], (NSEC, NPY, NPX), 0, 4) < 3).astype(jnp.int32), jax.random.fold_in(arg_keys[2], 1), 0, 1),
    }


def round_half(values):
    return lax.optimization_barrier(values.astype(jnp.bfloat16)).astype(jnp.float32)

def dft_tables(length):
    index = jnp.arange(length, dtype=jnp.int32)
    phase = (index[:, None] * index[None, :] % length).astype(jnp.float32) * (2.0 * math.pi / length)
    return (round_half(jnp.cos(phase)), round_half(jnp.sin(phase)))

def fit_basis(width):
    offsets = (jnp.arange(width, dtype=jnp.int32) - width // 2).astype(jnp.float32)
    ones = jnp.ones((width,), jnp.float32)
    square = offsets * offsets - jnp.mean(offsets * offsets)
    funcs = jnp.stack([ones[:, None] * ones[None, :], offsets[:, None] * ones[None, :], ones[:, None] * offsets[None, :], square[:, None] * ones[None, :], ones[:, None] * square[None, :], offsets[:, None] * offsets[None, :]], 0)
    return funcs / jnp.sqrt(lax.optimization_barrier(jnp.sum(funcs * funcs, axis=(1, 2), keepdims=True)))

def correlate_row(block, peak_row, valid_row):
    count = block.shape[0]
    length = block.shape[1]
    half = length // 2
    tiles = block.shape[2] // half - 1
    cosine, sine = dft_tables(length)
    columns = block.reshape(count, length, tiles + 1, half)
    patches = jnp.concatenate([columns[:, :, :-1], columns[:, :, 1:]], axis=3).astype(jnp.float32)
    energy = lax.optimization_barrier(jnp.mean(patches * patches, axis=(1, 3)))
    first_table = jnp.concatenate([cosine, -sine], 0)
    segment_one = round_half(jnp.einsum('cnjm,km->cnjk', patches, first_table))
    second_table = jnp.stack([jnp.stack([cosine, sine], 1), jnp.stack([-sine, cosine], 1)], 0).reshape(2 * length, 2, length)
    spectrum = round_half(jnp.einsum('qrn,cnjrk->cqjk', second_table, segment_one.reshape(count, length, tiles, 2, length)))
    real = spectrum[:, :length]
    imaginary = spectrum[:, length:]
    cross_real = real[:-1] * real[1:] + imaginary[:-1] * imaginary[1:]
    cross_imag = real[:-1] * imaginary[1:] - imaginary[:-1] * real[1:]
    cross = round_half(jnp.stack([cross_real, cross_imag], 1))
    third_table = jnp.stack([jnp.stack([cosine, -sine], 1), jnp.stack([sine, cosine], 1)], 0).reshape(2 * length, 2, length)
    inverse_one = round_half(jnp.einsum('qrn,crnjk->cqjk', third_table, cross))
    fourth_table = jnp.stack([cosine, -sine], 0)
    surface = jnp.einsum('crajk,rdk->cajd', inverse_one.reshape(count - 1, 2, length, tiles, length), fourth_table)
    scale = float(length) ** 3 * jnp.sqrt((energy[:-1] + 1e-05) * (energy[1:] + 1e-05))
    corr = surface / scale[:, None, :, None]
    height = lax.optimization_barrier(jnp.max(jnp.abs(corr), axis=(1, 3))) + 1e-05
    offsets = jnp.arange(WIN, dtype=jnp.int32) - WIN // 2
    positions = jnp.arange(length, dtype=jnp.int32)
    row_pick = (peak_row[:, 0, :, None] + offsets) % length
    col_pick = (peak_row[:, 1, :, None] + offsets) % length
    row_hot = (row_pick[..., None] == positions).astype(jnp.float32)
    col_hot = (col_pick[..., None] == positions).astype(jnp.float32)
    partial_rows = jnp.einsum('cjup,cpjq->cjuq', row_hot, corr, precision=lax.Precision.HIGHEST)
    window = jnp.einsum('cjuq,cjvq->cjuv', partial_rows, col_hot, precision=lax.Precision.HIGHEST)
    coefficient = jnp.einsum('euv,cjuv->cej', fit_basis(WIN), window, precision=lax.Precision.HIGHEST)
    return coefficient / height[:, None, :] * valid_row[:, None, :].astype(jnp.float32)

def reference(sections, peaks, valid):
    blank = jnp.zeros((1,) + sections.shape[1:], jnp.bfloat16)
    stacked = jnp.concatenate([sections, blank], 0)
    padded = jnp.pad(stacked, ((0, 0), (0, STRIDE), (0, STRIDE)))

    def one_row(index):
        block = lax.dynamic_slice_in_dim(padded, index * STRIDE, PATCH, axis=1)
        peak_row = lax.dynamic_index_in_dim(peaks, index, 2, False)
        valid_row = lax.dynamic_index_in_dim(valid, index, 1, False)
        return correlate_row(block, peak_row, valid_row)
    result = lax.map(one_row, jnp.arange(NPY, dtype=jnp.int32))
    return jnp.transpose(result, (1, 2, 0, 3))
```

```python
import functools
import math

import jax
import jax.numpy as jnp
import ml_dtypes
import numpy as np
from jax import lax
from jax.experimental import pallas as pl
from jax.experimental.pallas import tpu as pltpu
from jax.sharding import PartitionSpec as P

PATCH = 128
STRIDE = 64
WIN = 5
HALF = 64
ROWS = 704
LANES = 768
BLOCKS = 5
PAIRS = 3
F32 = jnp.float32
BF16 = jnp.bfloat16


def host_tables():
    index = np.arange(PATCH)
    phase = ((index[:, None] * index[None, :]) % PATCH).astype(np.float32) * np.float32(
        2.0 * math.pi / PATCH
    )
    rounded = lambda v: v.astype(ml_dtypes.bfloat16).astype(np.float32)
    cosine, sine = rounded(np.cos(phase)), rounded(np.sin(phase))
    first = np.zeros((256, 256), np.float32)
    last = np.zeros((256, 256), np.float32)
    weight = np.where(np.arange(HALF) == 0, 1.0, 2.0).astype(np.float32)
    for w in range(2):
        rows = slice(64 * w, 64 * w + 128)
        real, imag = slice(64 * w, 64 * w + 64), slice(128 + 64 * w, 192 + 64 * w)
        lags = slice(128 * w, 128 * w + 128)
        first[rows, real] = cosine[:HALF].T
        first[rows, imag] = -sine[:HALF].T
        first[rows, 128 + 64 * w] = 0.0
        last[real, lags] = (cosine[:, :HALF] * weight).T
        last[imag, lags] = (-sine[:, :HALF] * weight).T
        last[128 + 64 * w, lags] = cosine[:, HALF]
    nyquist = np.zeros((LANES, 128), np.float32)
    for b in range(BLOCKS):
        for w in range(2):
            start = 128 * b + 64 * w
            nyquist[start : start + 128, b + 64 * w] = cosine[HALF]
    forward = np.block([[cosine, sine], [-sine, cosine]])
    inverse = np.block([[cosine, -sine], [sine, cosine]])
    offsets = np.arange(WIN, dtype=np.float32) - WIN // 2
    ones = np.ones(WIN, np.float32)
    square = offsets * offsets - np.mean(offsets * offsets)
    pairs = [(ones, ones), (offsets, ones), (ones, offsets), (square, ones), (ones, square), (offsets, offsets)]
    basis = np.zeros((6, 8, 128), np.float32)
    for e, (p, q) in enumerate(pairs):
        func = p[:, None] * q[None, :]
        func = func / np.sqrt(np.sum(func * func))
        for j in range(2 * BLOCKS):
            basis[e, :WIN, 8 * j : 8 * j + WIN] = func
    gather = np.zeros((128, 128), np.float32)
    for j in range(2 * BLOCKS):
        gather[8 * j : 8 * j + 8, j] = 1.0
    spread = np.zeros((LANES, 128), np.float32)
    for j in range(2 * BLOCKS):
        spread[64 * j : 64 * j + 128, j] = 1.0
    low = lambda v: v.astype(ml_dtypes.bfloat16)
    return low(first), low(nyquist), low(forward), low(inverse), low(last), basis, gather, spread


def dot(a, b, precision=None):
    return lax.dot_general(a, b, (((1,), (0,)), ((), ())), precision=precision, preferred_element_type=F32)


def row_transform(x, first_ref, nyquist_ref, real_ref, imag_ref, rows):
    for b in range(BLOCKS):
        out = dot(x[:, 128 * b : 128 * b + 256], first_ref[...])
        real_ref[rows, 128 * b : 128 * b + 128] = out[:, :128].astype(BF16)
        imag_ref[rows, 128 * b : 128 * b + 128] = out[:, 128:].astype(BF16)
    b = BLOCKS
    real_ref[rows, 128 * b : 128 * b + 128] = dot(x, nyquist_ref[...]).astype(BF16)
    imag_ref[rows, 128 * b : 128 * b + 128] = jnp.zeros((x.shape[0], 128), BF16)


def square_sums(x, sums_ref, strip):
    x = x.astype(F32)
    sums_ref[pl.ds(strip, 1), :] = jnp.sum(x * x, axis=0, keepdims=True)


def column_transform(real_ref, imag_ref, start, pair, forward_ref):
    lanes = slice(256 * pair, 256 * pair + 256)
    data = jnp.concatenate([real_ref[pl.ds(start, 128), lanes], imag_ref[pl.ds(start, 128), lanes]], 0)
    return dot(forward_ref[...], data).astype(BF16)


def kernel(peaks_ref, own_ref, next_ref, first_ref, nyquist_ref, forward_ref, inverse_ref, last_ref,
           basis_ref, gather_ref, spread_ref, out_ref,
           own_re, own_im, next_re, next_im, own_sums, next_sums, back_re, back_im, surface, windows, peak_rows):
    def first_pass(strip, carry):
        rows = pl.ds(pl.multiple_of(strip * STRIDE, STRIDE), STRIDE)
        for x_ref, re, im, sums in ((own_ref, own_re, own_im, own_sums), (next_ref, next_re, next_im, next_sums)):
            x = x_ref[rows, :]
            square_sums(x, sums, strip)
            row_transform(x, first_ref, nyquist_ref, re, im, rows)
        return carry

    lax.fori_loop(0, ROWS // STRIDE, first_pass, 0)
    lane = lax.broadcasted_iota(jnp.int32, (128, 128), 1)
    slot = lax.rem(lane, HALF) == 0
    lane8 = lax.broadcasted_iota(jnp.int32, (8, 128), 1) // 8

    def patch_row(i, carry):
        start = pl.multiple_of(i * STRIDE, STRIDE)
        for pair in range(PAIRS):
            a = column_transform(own_re, own_im, start, pair, forward_ref).astype(F32)
            b = column_transform(next_re, next_im, start, pair, forward_ref).astype(F32)
            ar, ai, br, bi = a[:128], a[128:], b[:128], b[128:]
            cross = jnp.concatenate([(ar * br + ai * bi).astype(BF16), (ar * bi - ai * br).astype(BF16)], 0)
            back = dot(inverse_ref[...], cross)
            lanes = slice(256 * pair, 256 * pair + 256)
            back_re[:, lanes] = back[:128]
            back_im[:, lanes] = back[128:]
        extra = back_re[:, 128 * BLOCKS : 128 * BLOCKS + 128]
        for b in range(BLOCKS):
            lanes = slice(128 * b, 128 * b + 128)
            moved = extra if b == 0 else pltpu.roll(extra, 128 - b, 1)
            imag = jnp.where(slot, moved, back_im[:, lanes]).astype(BF16)
            data = jnp.concatenate([back_re[:, lanes].astype(BF16), imag], 1)
            out = dot(data, last_ref[...])
            for w in range(2):
                part = out[:, 128 * w : 128 * w + 128]
                j = 2 * b + w
                surface[j, 8:136, :] = part
                surface[j, 0:8, :] = part[120:]
                surface[j, 136:144, :] = part[:8]
                peak_rows[j, pl.ds(i, 1), :] = jnp.max(jnp.abs(part), axis=0, keepdims=True)
        held = jnp.zeros((8, 128), F32)
        for j in range(2 * BLOCKS):
            dy = peaks_ref[i, 0, j]
            dx = peaks_ref[i, 1, j]
            piece = surface[j, pl.ds(dy + 6, 8), :]
            shift = lax.rem(8 * j + 2 + 128 - dx, 128)
            held = jnp.where(lane8 == j, pltpu.roll(piece, shift, 1), held)
        windows[i] = held
        return carry

    lax.fori_loop(0, 10, patch_row, 0)
    finish(windows, peak_rows, own_sums, next_sums, basis_ref, gather_ref, spread_ref, out_ref)


def finish(windows, peak_rows, own_sums, next_sums, basis_ref, gather_ref, spread_ref, out_ref):
    high = lax.Precision.HIGHEST
    energy = []
    for sums in (own_sums, next_sums):
        joined = sums[0:10, :] + sums[1:11, :]
        energy.append(dot(joined, spread_ref[...], high) / float(PATCH * PATCH))
    scale = float(PATCH) ** 3 * jnp.sqrt((energy[0] + 1e-05) * (energy[1] + 1e-05))
    lane = lax.broadcasted_iota(jnp.int32, (10, 128), 1)
    peak = jnp.zeros((10, 128), F32)
    for j in range(2 * BLOCKS):
        peak = jnp.where(lane == j, jnp.max(peak_rows[j, 0:10, :], axis=1, keepdims=True), peak)
    height = peak / scale + 1e-05
    for e in range(6):
        rows = jnp.sum(windows[...] * basis_ref[e][None], axis=1)
        value = dot(rows, gather_ref[...], high) / scale / height
        out_ref[e, :, 0, :] = value[:, :10]


def correlate(peaks, own, following):
    tables = host_tables()
    vmem = pl.BlockSpec(memory_space=pltpu.VMEM)
    return pl.pallas_call(
        kernel,
        out_shape=jax.ShapeDtypeStruct((6, 10, 1, 10), F32),
        in_specs=[pl.BlockSpec(memory_space=pltpu.SMEM)] + [vmem] * (2 + len(tables)),
        out_specs=vmem,
        scratch_shapes=[
            pltpu.VMEM((ROWS, LANES), BF16),
            pltpu.VMEM((ROWS, LANES), BF16),
            pltpu.VMEM((ROWS, LANES), BF16),
            pltpu.VMEM((ROWS, LANES), BF16),
            pltpu.VMEM((16, LANES), F32),
            pltpu.VMEM((16, LANES), F32),
            pltpu.VMEM((128, LANES), F32),
            pltpu.VMEM((128, LANES), F32),
            pltpu.VMEM((10, 144, 128), F32),
            pltpu.VMEM((10, 8, 128), F32),
            pltpu.VMEM((10, 16, 128), F32),
        ],
        compiler_params=pltpu.CompilerParams(vmem_limit_bytes=56 * 1024 * 1024),
    )(peaks, own, following, *[jnp.asarray(t) for t in tables])


def passed_along(value, axis, steps):
    count = lax.axis_size(axis)
    initial, last = (max(0, -steps), min(count, count - steps))
    return lax.ppermute(value, axis, [(source, source + steps) for source in range(initial, last)])


def body(sections, peaks, valid):
    tile = sections[0]
    lower = passed_along(tile[:STRIDE, :], "gy", -1)
    taller = jnp.concatenate([tile, lower], 0)
    beside = passed_along(taller[:, :STRIDE], "gx", -1)
    extended = jnp.concatenate([taller, beside, jnp.zeros((ROWS, LANES - ROWS), BF16)], 1)
    following = passed_along(extended, "gz", -1)
    out = correlate(jnp.transpose(peaks, (0, 2, 1, 3))[0], extended, following)
    return jnp.transpose(out, (2, 0, 1, 3)) * valid[:, None].astype(F32)


def solution(mesh):
    in_specs = (P("gz", "gy", "gx"), P("gz", None, "gy", "gx"), P("gz", "gy", "gx"))
    out_specs = P("gz", None, "gy", "gx")
    return jax.shard_map(body, mesh=mesh, in_specs=in_specs, out_specs=out_specs, check_vma=False)
```

```python
import functools
import math

import jax
import jax.numpy as jnp
import ml_dtypes
import numpy as np
from jax import lax
from jax.experimental import pallas as pl
from jax.experimental.pallas import tpu as pltpu
from jax.sharding import PartitionSpec as P

PATCH = 128
STRIDE = 64
WIN = 5
HALF = 64
ROWS = 704
LANES = 768
BLOCKS = 5
PAIRS = 3
CHUNKS = 6
PART_ROWS = CHUNKS * STRIDE
F32 = jnp.float32
BF16 = jnp.bfloat16


def host_tables():
    index = np.arange(PATCH)
    phase = ((index[:, None] * index[None, :]) % PATCH).astype(np.float32) * np.float32(
        2.0 * math.pi / PATCH
    )
    rounded = lambda v: v.astype(ml_dtypes.bfloat16).astype(np.float32)
    cosine, sine = rounded(np.cos(phase)), rounded(np.sin(phase))
    first = np.zeros((256, 256), np.float32)
    last = np.zeros((256, 256), np.float32)
    weight = np.where(np.arange(HALF) == 0, 1.0, 2.0).astype(np.float32)
    for w in range(2):
        rows = slice(64 * w, 64 * w + 128)
        real, imag = slice(64 * w, 64 * w + 64), slice(128 + 64 * w, 192 + 64 * w)
        lags = slice(128 * w, 128 * w + 128)
        first[rows, real] = cosine[:HALF].T
        first[rows, imag] = -sine[:HALF].T
        first[rows, 128 + 64 * w] = 0.0
        last[real, lags] = (cosine[:, :HALF] * weight).T
        last[imag, lags] = (-sine[:, :HALF] * weight).T
        last[128 + 64 * w, lags] = cosine[:, HALF]
    nyquist = np.zeros((LANES, 128), np.float32)
    for b in range(BLOCKS):
        for w in range(2):
            start = 128 * b + 64 * w
            nyquist[start : start + 128, b + 64 * w] = cosine[HALF]
    forward = np.block([[cosine, sine], [-sine, cosine]])
    inverse = np.stack([np.block([[cosine, sine], [sine, -cosine]]), np.block([[cosine, -sine], [sine, cosine]])])
    offsets = np.arange(WIN, dtype=np.float32) - WIN // 2
    ones = np.ones(WIN, np.float32)
    square = offsets * offsets - np.mean(offsets * offsets)
    pairs = [(ones, ones), (offsets, ones), (ones, offsets), (square, ones), (ones, square), (offsets, offsets)]
    basis = np.zeros((6, 8, 128), np.float32)
    for e, (p, q) in enumerate(pairs):
        func = p[:, None] * q[None, :]
        func = func / np.sqrt(np.sum(func * func))
        for j in range(2 * BLOCKS):
            basis[e, :WIN, 8 * j : 8 * j + WIN] = func
    gather = np.zeros((128, 128), np.float32)
    for j in range(2 * BLOCKS):
        gather[8 * j : 8 * j + 8, j] = 1.0
    spread = np.zeros((LANES, 128), np.float32)
    for j in range(2 * BLOCKS):
        spread[64 * j : 64 * j + 128, j] = 1.0
    low = lambda v: v.astype(ml_dtypes.bfloat16)
    return low(first), low(nyquist), low(forward), low(inverse), low(last), basis, gather, spread


def dot(a, b, precision=None):
    return lax.dot_general(a, b, (((1,), (0,)), ((), ())), precision=precision, preferred_element_type=F32)


def row_transform(x, first_ref, nyquist_ref, real_ref, imag_ref, rows):
    for b in range(BLOCKS):
        out = dot(x[:, 128 * b : 128 * b + 256], first_ref[...])
        real_ref[rows, 128 * b : 128 * b + 128] = out[:, :128].astype(BF16)
        imag_ref[rows, 128 * b : 128 * b + 128] = out[:, 128:].astype(BF16)
    b = BLOCKS
    real_ref[rows, 128 * b : 128 * b + 128] = dot(x, nyquist_ref[...]).astype(BF16)
    imag_ref[rows, 128 * b : 128 * b + 128] = jnp.zeros((x.shape[0], 128), BF16)


def square_sums(x, sums_ref, strip):
    x = x.astype(F32)
    sums_ref[pl.ds(strip, 1), :] = jnp.sum(x * x, axis=0, keepdims=True)


def column_transform(real_ref, imag_ref, start, pair, forward_ref):
    lanes = slice(256 * pair, 256 * pair + 256)
    data = jnp.concatenate([real_ref[pl.ds(start, 128), lanes], imag_ref[pl.ds(start, 128), lanes]], 0)
    return dot(forward_ref[...], data).astype(BF16)


MAIN = 640
BEFORE, AFTER = 0, 1


class Place:
    def __init__(self):
        self.at = {name: lax.axis_index(name) for name in ("gz", "gx", "gy")}
        self.size = {name: lax.axis_size(name) for name in ("gz", "gx", "gy")}

    def there(self, step):
        inside = None
        for name, move in zip(("gz", "gx", "gy"), step):
            if move:
                ok = self.at[name] + move < self.size[name] if move > 0 else self.at[name] + move >= 0
                inside = ok if inside is None else jnp.logical_and(inside, ok)
        return inside

    def device(self, step):
        return {name: self.at[name] + move for name, move in zip(("gz", "gx", "gy"), step)}


def back(step):
    return tuple(-move for move in step)


def kernel(tile_ref, peaks_ref, first_hbm, nyquist_hbm, forward_hbm, inverse_hbm, last_hbm, basis_hbm, gather_hbm, spread_hbm,
           out_ref,
           own, other, first_ref, nyquist_ref, forward_ref, inverse_ref, last_ref, basis_ref, gather_ref, spread_ref,
           own_re, own_im, other_re, other_im, spectra, own_sums, other_sums, back_re, back_im, surface, windows, peak_rows,
           result, returned, far_peaks, peaks, local_sems, send_sems, recv_sems):
    place = Place()
    tables = [(first_hbm, first_ref), (nyquist_hbm, nyquist_ref), (forward_hbm, forward_ref), (inverse_hbm, inverse_ref),
              (last_hbm, last_ref), (basis_hbm, basis_ref), (gather_hbm, gather_ref), (spread_hbm, spread_ref)]
    main, edge = pl.ds(0, MAIN), pl.ds(MAIN, 128)
    tile_copy = pltpu.make_async_copy(tile_ref, own.at[pl.ds(0, MAIN), main], local_sems.at[0])
    local = [pltpu.make_async_copy(peaks_ref.at[pl.ds(0, 5)], peaks.at[AFTER], local_sems.at[1])]
    local += [pltpu.make_async_copy(a, b, local_sems.at[2 + n]) for n, (a, b) in enumerate(tables)]
    tile_copy.start()
    for copy in local:
        copy.start()

    top = pl.ds(0, STRIDE)
    low = pl.ds(MAIN, STRIDE)
    left = pl.ds(0, 128)
    copies = [
        ((0, -1, 0), tile_ref.at[:, left], own.at[pl.ds(0, MAIN), edge]),
        ((0, 0, -1), tile_ref.at[top, :], own.at[low, main]),
        ((0, -1, -1), tile_ref.at[top, left], own.at[low, edge]),
        ((1, 0, 0), peaks_ref.at[pl.ds(5, 5)], far_peaks),
        ((-1, 0, 0), result, returned),
    ]
    early, ret = len(copies) - 1, len(copies) - 1
    parts = {}
    for c in range(CHUNKS):
        rows = pl.ds(STRIDE * c, STRIDE)
        for part in (BEFORE, AFTER):
            for columns, source_columns, shift in ((main, main, 0), (edge, left, -1)):
                move = -1 if part == AFTER else 1
                if part == BEFORE and c == CHUNKS - 1:
                    step, source = (move, shift, -1), top
                else:
                    step = (move, shift, 0)
                    source = rows if part == AFTER else pl.ds(MAIN - PART_ROWS + STRIDE + STRIDE * c, STRIDE)
                parts[c, part, shift] = len(copies)
                copies.append((step, tile_ref.at[source, source_columns], other.at[part, rows, columns]))

    def remote(n):
        step, source, destination = copies[n]
        return pltpu.make_async_remote_copy(
            src_ref=source, dst_ref=destination, send_sem=send_sems.at[n], recv_sem=recv_sems.at[n],
            device_id=place.device(step), device_id_type=pl.DeviceIdType.MESH,
        )

    def wait_for(n):
        pl.when(place.there(back(copies[n][0])))(lambda: remote(n).wait_recv())

    @pl.when(place.at["gy"] == place.size["gy"] - 1)
    def _():
        own[MAIN:ROWS, :] = jnp.zeros((STRIDE, LANES), BF16)
        other[BEFORE, PART_ROWS - STRIDE :, :] = jnp.zeros((STRIDE, LANES), BF16)

    @pl.when(place.at["gx"] == place.size["gx"] - 1)
    def _():
        own[:, MAIN:] = jnp.zeros((ROWS, LANES - MAIN), BF16)
        for part in (BEFORE, AFTER):
            other[part, :, MAIN:] = jnp.zeros((PART_ROWS, LANES - MAIN), BF16)

    @pl.when(place.at["gz"] == place.size["gz"] - 1)
    def _():
        other[AFTER] = jnp.zeros((PART_ROWS, LANES), BF16)
        returned[...] = jnp.zeros_like(returned)

    @pl.when(place.at["gz"] == 0)
    def _():
        other[BEFORE] = jnp.zeros((PART_ROWS, LANES), BF16)
        far_peaks[...] = jnp.zeros_like(far_peaks)

    barrier = pltpu.get_barrier_semaphore()
    steps = sorted({step for step, _, _ in copies})
    for step in steps:
        @pl.when(place.there(back(step)))
        def _():
            pl.semaphore_signal(barrier, inc=1, device_id=place.device(back(step)), device_id_type=pl.DeviceIdType.MESH)
    pl.semaphore_wait(barrier, sum(place.there(step).astype(jnp.int32) for step in steps))
    for n in range(len(copies)):
        if n != ret:
            pl.when(place.there(copies[n][0]))(lambda: remote(n).start())

    tile_copy.wait()
    for copy in local:
        copy.wait()
    for n in range(3):
        wait_for(n)

    def own_rows(strip, carry):
        rows = pl.ds(pl.multiple_of(strip * STRIDE, STRIDE), STRIDE)
        x = own[rows, :]
        square_sums(x, own_sums, strip)
        row_transform(x, first_ref, nyquist_ref, own_re, own_im, rows)
        return carry

    lax.fori_loop(0, ROWS // STRIDE, own_rows, 0)

    def own_spectra(i, carry):
        start = pl.multiple_of(i * STRIDE, STRIDE)
        for pair in range(PAIRS):
            spectra[i, pair] = column_transform(own_re, own_im, start, pair, forward_ref)
        return carry

    lax.fori_loop(0, 10, own_spectra, 0)
    wait_for(3)
    far = pltpu.make_async_copy(far_peaks, peaks.at[BEFORE], local_sems.at[1])
    far.start()
    far.wait()

    lane = lax.broadcasted_iota(jnp.int32, (128, 128), 1)
    slot = lax.rem(lane, HALF) == 0
    lane8 = lax.broadcasted_iota(jnp.int32, (8, 128), 1) // 8

    def wait_chunk(c, part):
        for shift in (0, -1):
            wait_for(parts[c, part, shift])

    def other_rows(c, part):
        rows = pl.ds(pl.multiple_of(c * STRIDE, STRIDE), STRIDE)
        x = other[part, rows, :]
        square_sums(x, other_sums.at[part], c)
        row_transform(x, first_ref, nyquist_ref, other_re.at[part], other_im.at[part], rows)

    def patch_row(i, part):
        start = pl.multiple_of(i * STRIDE, STRIDE)
        row = jnp.where(part == BEFORE, 5, 0) + i
        for pair in range(PAIRS):
            a = spectra[row, pair].astype(F32)
            b = column_transform(other_re.at[part], other_im.at[part], start, pair, forward_ref).astype(F32)
            ar, ai, br, bi = a[:128], a[128:], b[:128], b[128:]
            cross = jnp.concatenate([(ar * br + ai * bi).astype(BF16), (ar * bi - ai * br).astype(BF16)], 0)
            turned = dot(inverse_ref[part], cross)
            lanes = slice(256 * pair, 256 * pair + 256)
            back_re[:, lanes] = turned[:128]
            back_im[:, lanes] = turned[128:]
        extra = back_re[:, 128 * BLOCKS : 128 * BLOCKS + 128]
        for b in range(BLOCKS):
            lanes = slice(128 * b, 128 * b + 128)
            moved = extra if b == 0 else pltpu.roll(extra, 128 - b, 1)
            imag = jnp.where(slot, moved, back_im[:, lanes]).astype(BF16)
            data = jnp.concatenate([back_re[:, lanes].astype(BF16), imag], 1)
            out = dot(data, last_ref[...])
            for w in range(2):
                piece = out[:, 128 * w : 128 * w + 128]
                j = 2 * b + w
                surface[j, 8:136, :] = piece
                surface[j, 0:8, :] = piece[120:]
                surface[j, 136:144, :] = piece[:8]
                peak_rows[part, j, pl.ds(i, 1), :] = jnp.max(jnp.abs(piece), axis=0, keepdims=True)
        held = jnp.zeros((8, 128), F32)
        for j in range(2 * BLOCKS):
            dy = peaks[part, i, 0, j]
            dx = peaks[part, i, 1, j]
            piece = surface[j, pl.ds(dy + 6, 8), :]
            shift = lax.rem(8 * j + 2 + 128 - dx, 128)
            held = jnp.where(lane8 == j, pltpu.roll(piece, shift, 1), held)
        windows[part, i] = held

    def finish(part):
        high = lax.Precision.HIGHEST
        first = 5 if part == BEFORE else 0
        joined = [own_sums[first : first + 5, :] + own_sums[first + 1 : first + 6, :],
                  other_sums[part, 0:5, :] + other_sums[part, 1:6, :]]
        energy = [dot(sums, spread_ref[...], high) / float(PATCH * PATCH) for sums in joined]
        scale = float(PATCH) ** 3 * jnp.sqrt((energy[0] + 1e-05) * (energy[1] + 1e-05))
        lane5 = lax.broadcasted_iota(jnp.int32, (5, 128), 1)
        peak = jnp.zeros((5, 128), F32)
        for j in range(2 * BLOCKS):
            peak = jnp.where(lane5 == j, jnp.max(peak_rows[part, j, 0:5, :], axis=1, keepdims=True), peak)
        height = peak / scale + 1e-05
        values = []
        for e in range(6):
            rows = jnp.sum(windows[part] * basis_ref[e][None], axis=1)
            values.append(dot(rows, gather_ref[...], high) / scale / height)
        return values

    for part in (BEFORE, AFTER):
        wait_chunk(0, part)
        other_rows(0, part)

    for c in range(1, CHUNKS):
        for part in (BEFORE, AFTER):
            wait_chunk(c, part)
        def both(part, carry):
            other_rows(c, part)
            patch_row(c - 1, part)
            return carry
        lax.fori_loop(0, 2, both, 0)

    for e, value in enumerate(finish(BEFORE)):
        result[e, 0:5, :] = value
    pl.when(place.there(copies[ret][0]))(lambda: remote(ret).start())
    for e, value in enumerate(finish(AFTER)):
        out_ref[e, 0:5, 0, :] = value[:, :10]
    wait_for(ret)
    for e in range(6):
        out_ref[e, 5:10, 0, :] = returned[e, 0:5, :10]
    for n in range(len(copies)):
        pl.when(place.there(copies[n][0]))(lambda: remote(n).wait_send())


def correlate(tile, peaks):
    tables = host_tables()
    anywhere = pl.BlockSpec(memory_space=pl.ANY)
    count = 5 + 4 * CHUNKS
    return pl.pallas_call(
        kernel,
        out_shape=jax.ShapeDtypeStruct((6, 10, 1, 10), F32),
        in_specs=[anywhere] * (2 + len(tables)),
        out_specs=pl.BlockSpec(memory_space=pltpu.VMEM),
        scratch_shapes=[
            pltpu.VMEM((ROWS, LANES), BF16),
            pltpu.VMEM((2, PART_ROWS, LANES), BF16),
            *[pltpu.VMEM(t.shape, t.dtype) for t in tables],
            pltpu.VMEM((ROWS, LANES), BF16),
            pltpu.VMEM((ROWS, LANES), BF16),
            pltpu.VMEM((2, PART_ROWS, LANES), BF16),
            pltpu.VMEM((2, PART_ROWS, LANES), BF16),
            pltpu.VMEM((10, PAIRS, 256, 256), BF16),
            pltpu.VMEM((16, LANES), F32),
            pltpu.VMEM((2, 8, LANES), F32),
            pltpu.VMEM((128, LANES), F32),
            pltpu.VMEM((128, LANES), F32),
            pltpu.VMEM((10, 144, 128), F32),
            pltpu.VMEM((2, 5, 8, 128), F32),
            pltpu.VMEM((2, 10, 8, 128), F32),
            pltpu.VMEM((6, 8, 128), F32),
            pltpu.VMEM((6, 8, 128), F32),
            pltpu.VMEM((5, 2, 10), jnp.int32),
            pltpu.SMEM((2, 5, 2, 10), jnp.int32),
            pltpu.SemaphoreType.DMA((2 + len(tables),)),
            pltpu.SemaphoreType.DMA((count,)),
            pltpu.SemaphoreType.DMA((count,)),
        ],
        compiler_params=pltpu.CompilerParams(
            collective_id=0, has_side_effects=True, vmem_limit_bytes=48 * 1024 * 1024
        ),
    )(tile, peaks, *[jnp.asarray(t) for t in tables])


def body(sections, peaks, valid):
    out = correlate(sections[0], jnp.transpose(peaks, (0, 2, 1, 3))[0])
    return jnp.transpose(out, (2, 0, 1, 3)) * valid[:, None].astype(F32)


def solution(mesh):
    in_specs = (P("gz", "gy", "gx"), P("gz", None, "gy", "gx"), P("gz", "gy", "gx"))
    out_specs = P("gz", None, "gy", "gx")
    return jax.shard_map(body, mesh=mesh, in_specs=in_specs, out_specs=out_specs, check_vma=False)
```

```python
import functools
import math

import jax
import jax.numpy as jnp
import ml_dtypes
import numpy as np
from jax import lax
from jax.experimental import pallas as pl
from jax.experimental.pallas import tpu as pltpu
from jax.sharding import PartitionSpec as P

PATCH = 128
STRIDE = 64
WIN = 5
HALF = 64
ROWS = 704
LANES = 768
BLOCKS = 5
PAIRS = 3
CHUNKS = 6
PART_ROWS = CHUNKS * STRIDE
F32 = jnp.float32
BF16 = jnp.bfloat16


def host_tables():
    index = np.arange(PATCH)
    phase = ((index[:, None] * index[None, :]) % PATCH).astype(np.float32) * np.float32(
        2.0 * math.pi / PATCH
    )
    rounded = lambda v: v.astype(ml_dtypes.bfloat16).astype(np.float32)
    cosine, sine = rounded(np.cos(phase)), rounded(np.sin(phase))
    first = np.zeros((256, 256), np.float32)
    last = np.zeros((256, 256), np.float32)
    weight = np.where(np.arange(HALF) == 0, 1.0, 2.0).astype(np.float32)
    for w in range(2):
        rows = slice(64 * w, 64 * w + 128)
        real, imag = slice(64 * w, 64 * w + 64), slice(128 + 64 * w, 192 + 64 * w)
        lags = slice(128 * w, 128 * w + 128)
        first[rows, real] = cosine[:HALF].T
        first[rows, imag] = -sine[:HALF].T
        first[rows, 128 + 64 * w] = 0.0
        last[real, lags] = (cosine[:, :HALF] * weight).T
        last[imag, lags] = (-sine[:, :HALF] * weight).T
        last[128 + 64 * w, lags] = cosine[:, HALF]
    nyquist = np.zeros((LANES, 128), np.float32)
    for b in range(BLOCKS):
        for w in range(2):
            start = 128 * b + 64 * w
            nyquist[start : start + 128, b + 64 * w] = cosine[HALF]
    forward = np.block([[cosine, sine], [-sine, cosine]])
    inverse = np.stack([np.block([[cosine, sine], [sine, -cosine]]), np.block([[cosine, -sine], [sine, cosine]])])
    offsets = np.arange(WIN, dtype=np.float32) - WIN // 2
    ones = np.ones(WIN, np.float32)
    square = offsets * offsets - np.mean(offsets * offsets)
    pairs = [(ones, ones), (offsets, ones), (ones, offsets), (square, ones), (ones, square), (offsets, offsets)]
    basis = np.zeros((6, 8, 128), np.float32)
    for e, (p, q) in enumerate(pairs):
        func = p[:, None] * q[None, :]
        func = func / np.sqrt(np.sum(func * func))
        for j in range(2 * BLOCKS):
            basis[e, :WIN, 8 * j : 8 * j + WIN] = func
    gather = np.zeros((128, 128), np.float32)
    for j in range(2 * BLOCKS):
        gather[8 * j : 8 * j + 8, j] = 1.0
    spread = np.zeros((LANES, 128), np.float32)
    for j in range(2 * BLOCKS):
        spread[64 * j : 64 * j + 128, j] = 1.0
    low = lambda v: v.astype(ml_dtypes.bfloat16)
    return low(first), low(nyquist), low(forward), low(inverse), low(last), basis, gather, spread


def dot(a, b, precision=None):
    return lax.dot_general(a, b, (((1,), (0,)), ((), ())), precision=precision, preferred_element_type=F32)


def row_transform(x, first_ref, block):
    return dot(x[:, 128 * block : 128 * block + 256], first_ref[...]).astype(BF16)


def unpack(packed):
    wide = packed.astype(F32)
    return jnp.concatenate([wide, pltpu.roll(wide, HALF, 1)], 0).astype(BF16)


def square_sums(x, sums_ref, strip):
    x = x.astype(F32)
    sums_ref[pl.ds(strip, 1), :] = jnp.sum(x * x, axis=0, keepdims=True)


def column_transform(real_ref, imag_ref, start, forward_ref):
    data = jnp.concatenate([real_ref[pl.ds(start, 128), :], imag_ref[pl.ds(start, 128), :]], 0)
    return dot(forward_ref[...], data).astype(BF16)


MAIN = 640
BEFORE, AFTER = 0, 1


class Place:
    def __init__(self):
        self.at = {name: lax.axis_index(name) for name in ("gz", "gx", "gy")}
        self.size = {name: lax.axis_size(name) for name in ("gz", "gx", "gy")}

    def there(self, step):
        inside = None
        for name, move in zip(("gz", "gx", "gy"), step):
            if move:
                ok = self.at[name] + move < self.size[name] if move > 0 else self.at[name] + move >= 0
                inside = ok if inside is None else jnp.logical_and(inside, ok)
        return inside

    def device(self, step):
        return {name: self.at[name] + move for name, move in zip(("gz", "gx", "gy"), step)}


def back(step):
    return tuple(-move for move in step)


def kernel(tile_ref, peaks_ref, first_hbm, nyquist_hbm, forward_hbm, inverse_hbm, last_hbm, basis_hbm, gather_hbm, spread_hbm,
           out_ref,
           own, other, packed, own_edge, other_edge,
           first_ref, nyquist_ref, forward_ref, inverse_ref, last_ref, basis_ref, gather_ref, spread_ref,
           own_re, own_im, other_re, other_im, spectra, own_sums, other_sums, surface, windows, peak_rows,
           result, returned, far_peaks, peaks, local_sems, send_sems, recv_sems):
    place = Place()
    tables = [(first_hbm, first_ref), (nyquist_hbm, nyquist_ref), (forward_hbm, forward_ref), (inverse_hbm, inverse_ref),
              (last_hbm, last_ref), (basis_hbm, basis_ref), (gather_hbm, gather_ref), (spread_hbm, spread_ref)]
    main = pl.ds(0, MAIN)
    tile_copy = pltpu.make_async_copy(tile_ref, own.at[main, main], local_sems.at[0])
    local = [pltpu.make_async_copy(peaks_ref.at[pl.ds(0, 5)], peaks.at[AFTER], local_sems.at[1])]
    local += [pltpu.make_async_copy(a, b, local_sems.at[2 + n]) for n, (a, b) in enumerate(tables)]
    tile_copy.start()
    for copy in local:
        copy.start()

    copies = [
        ((0, 0, -1), tile_ref.at[pl.ds(0, STRIDE), :], own.at[pl.ds(MAIN, STRIDE), main]),
        ((0, -1, 0), packed, own_edge.at[pl.ds(0, MAIN // 2)]),
        ((0, -1, -1), packed.at[pl.ds(0, 32)], own_edge.at[pl.ds(MAIN // 2, 32)]),
        ((1, 0, 0), peaks_ref.at[pl.ds(5, 5)], far_peaks),
        ((-1, 0, 0), result, returned),
    ]
    ret = len(copies) - 1
    base = len(copies)
    for c in range(CHUNKS):
        for part in (BEFORE, AFTER):
            move = -1 if part == AFTER else 1
            strip = c if part == AFTER else (5 + c) % 10
            low = -1 if part == BEFORE and c == CHUNKS - 1 else 0
            rows = pl.ds(STRIDE * c, STRIDE)
            copies.append(((move, 0, low), tile_ref.at[pl.ds(STRIDE * strip, STRIDE), :], other.at[part, rows, :]))
            copies.append(((move, -1, low), packed.at[pl.ds(32 * strip, 32)], other_edge.at[part, pl.ds(32 * c, 32)]))

    def remote(n):
        step, source, destination = copies[n]
        return pltpu.make_async_remote_copy(
            src_ref=source, dst_ref=destination, send_sem=send_sems.at[n], recv_sem=recv_sems.at[n],
            device_id=place.device(step), device_id_type=pl.DeviceIdType.MESH,
        )

    def wait_for(n):
        pl.when(place.there(back(copies[n][0])))(lambda: remote(n).wait_recv())

    @pl.when(place.at["gy"] == place.size["gy"] - 1)
    def _():
        own[MAIN:ROWS, :MAIN] = jnp.zeros((STRIDE, MAIN), BF16)
        own_edge[MAIN // 2 :, :] = jnp.zeros((32, 128), BF16)
        other[BEFORE, PART_ROWS - STRIDE :, :] = jnp.zeros((STRIDE, MAIN), BF16)
        other_edge[BEFORE, PART_ROWS // 2 - 32 :, :] = jnp.zeros((32, 128), BF16)

    @pl.when(place.at["gx"] == place.size["gx"] - 1)
    def _():
        own_edge[...] = jnp.zeros_like(own_edge)
        other_edge[...] = jnp.zeros_like(other_edge)

    @pl.when(place.at["gz"] == place.size["gz"] - 1)
    def _():
        other[AFTER] = jnp.zeros((PART_ROWS, MAIN), BF16)
        other_edge[AFTER] = jnp.zeros((PART_ROWS // 2, 128), BF16)
        returned[...] = jnp.zeros_like(returned)

    @pl.when(place.at["gz"] == 0)
    def _():
        other[BEFORE] = jnp.zeros((PART_ROWS, MAIN), BF16)
        other_edge[BEFORE] = jnp.zeros((PART_ROWS // 2, 128), BF16)
        far_peaks[...] = jnp.zeros_like(far_peaks)

    lane = lax.broadcasted_iota(jnp.int32, (128, 128), 1)
    slot = lax.rem(lane, HALF) == 0
    lane8 = lax.broadcasted_iota(jnp.int32, (8, 128), 1) // 8
    left = lax.broadcasted_iota(jnp.int32, (32, 128), 1) < HALF

    barrier = pltpu.get_barrier_semaphore()
    steps = sorted({step for step, _, _ in copies})
    for step in steps:
        @pl.when(place.there(back(step)))
        def _():
            pl.semaphore_signal(barrier, inc=1, device_id=place.device(back(step)), device_id_type=pl.DeviceIdType.MESH)
    tile_copy.wait()
    for n in range(MAIN // STRIDE):
        block = own[STRIDE * n : STRIDE * n + STRIDE, 0:128].astype(F32)
        packed[32 * n : 32 * n + 32, :] = jnp.where(left, block[:32], pltpu.roll(block[32:], HALF, 1)).astype(BF16)
    pl.semaphore_wait(barrier, sum(place.there(step).astype(jnp.int32) for step in steps))
    for n in range(len(copies)):
        if n != ret:
            pl.when(place.there(copies[n][0]))(lambda: remote(n).start())

    windows[...] = jnp.zeros_like(windows)
    peak_rows[...] = jnp.zeros_like(peak_rows)
    for copy in local:
        copy.wait()

    def keep(re, im, rows, b, out):
        re[rows, 128 * b : 128 * b + 128] = out[:, :128]
        im[rows, 128 * b : 128 * b + 128] = out[:, 128:]

    def keep_nyquist(re, im, rows, out):
        re[rows, 128 * BLOCKS :] = out
        im[rows, 128 * BLOCKS :] = jnp.zeros((out.shape[0], 128), BF16)

    for b in range(BLOCKS - 1):
        keep(own_re, own_im, slice(0, MAIN), b, row_transform(own[0:MAIN, :], first_ref, b))
    for n in range(3):
        wait_for(n)

    def own_strip(strip, carry):
        rows = pl.ds(pl.multiple_of(strip * STRIDE, STRIDE), STRIDE)
        own[rows, MAIN:] = unpack(own_edge[pl.ds(pl.multiple_of(strip * 32, 32), 32), :])
        square_sums(own[rows, :], own_sums, strip)
        return carry

    lax.fori_loop(0, ROWS // STRIDE, own_strip, 0)
    for b in range(BLOCKS - 1):
        keep(own_re, own_im, slice(MAIN, ROWS), b, row_transform(own[MAIN:ROWS, :], first_ref, b))
    keep(own_re, own_im, slice(0, ROWS), BLOCKS - 1, row_transform(own[...], first_ref, BLOCKS - 1))
    keep_nyquist(own_re, own_im, slice(0, ROWS), dot(own[...], nyquist_ref[...]).astype(BF16))

    def own_spectra(i, carry):
        for half in range(2):
            row = 5 * half + i
            spectra[row] = column_transform(own_re, own_im, pl.multiple_of(row * STRIDE, STRIDE), forward_ref)
        return carry

    lax.fori_loop(0, 5, own_spectra, 0)
    wait_for(3)
    far = pltpu.make_async_copy(far_peaks, peaks.at[BEFORE], local_sems.at[1])
    far.start()
    far.wait()

    both = (BEFORE, AFTER)

    def wait_chunk(c):
        rows = pl.ds(pl.multiple_of(c * STRIDE, STRIDE), STRIDE)
        half = pl.ds(pl.multiple_of(c * 32, 32), 32)
        for part in both:
            there = place.there((1, 0, 0)) if part == AFTER else jnp.logical_and(
                place.there((-1, 0, 0)), jnp.logical_or(c < CHUNKS - 1, place.there((0, 0, 1))))
            beside = jnp.logical_and(there, place.there((0, 1, 0)))
            n = base + 4 * c + 2 * part
            for k, (ok, ref) in enumerate(((there, other.at[part, rows, :]), (beside, other_edge.at[part, half]))):
                @pl.when(ok)
                def _():
                    pltpu.make_async_remote_copy(
                        src_ref=ref, dst_ref=ref, send_sem=send_sems.at[n + k], recv_sem=recv_sems.at[n + k],
                        device_id=place.device((0, 0, 0)), device_id_type=pl.DeviceIdType.MESH,
                    ).wait_recv()

    def other_rows(c):
        rows = pl.ds(pl.multiple_of(c * STRIDE, STRIDE), STRIDE)
        half = pl.ds(pl.multiple_of(c * 32, 32), 32)
        pieces = [jnp.concatenate([other[part, rows, :], unpack(other_edge[part, half, :])], 1) for part in both]
        x = jnp.concatenate(pieces, 0)
        for b in range(BLOCKS):
            out = row_transform(x, first_ref, b)
            for part in both:
                keep(other_re.at[part], other_im.at[part], rows, b, out[64 * part : 64 * part + 64])
        out = dot(x, nyquist_ref[...]).astype(BF16)
        for part in both:
            keep_nyquist(other_re.at[part], other_im.at[part], rows, out[64 * part : 64 * part + 64])
            square_sums(pieces[part], other_sums.at[part], c)

    def patch_rows(i):
        start = pl.multiple_of(i * STRIDE, STRIDE)
        crosses = []
        for part in both:
            a = spectra[(5 if part == BEFORE else 0) + i].astype(F32)
            b = column_transform(other_re.at[part], other_im.at[part], start, forward_ref).astype(F32)
            ar, ai, br, bi = a[:128], a[128:], b[:128], b[128:]
            crosses.append(jnp.concatenate([(ar * br + ai * bi).astype(BF16), (ar * bi - ai * br).astype(BF16)], 0))
        for part in both:
            turned = dot(inverse_ref[part], crosses[part])
            extra = turned[:128, 128 * BLOCKS :]
            for b in range(BLOCKS):
                lanes = slice(128 * b, 128 * b + 128)
                moved = extra if b == 0 else pltpu.roll(extra, 128 - b, 1)
                imag = jnp.where(slot, moved, turned[128:, lanes]).astype(BF16)
                out = dot(jnp.concatenate([turned[:128, lanes].astype(BF16), imag], 1), last_ref[...])
                for w in range(2):
                    piece = out[:, 128 * w : 128 * w + 128]
                    j = 2 * b + w
                    surface[part, j, 8:136, :] = piece
                    surface[part, j, 0:8, :] = piece[120:]
                    surface[part, j, 136:144, :] = piece[:8]
                    peak_rows[part, j, pl.ds(i, 1), :] = jnp.max(jnp.abs(piece), axis=0, keepdims=True)
        for part in both:
            held = jnp.zeros((8, 128), F32)
            for j in range(2 * BLOCKS):
                dy = peaks[part, i, 0, j]
                dx = peaks[part, i, 1, j]
                piece = surface[part, j, pl.ds(dy + 6, 8), :]
                shift = lax.rem(8 * j + 2 + 128 - dx, 128)
                held = jnp.where(lane8 == j, pltpu.roll(piece, shift, 1), held)
            windows[part, i] = held

    high = lax.Precision.HIGHEST

    def energy(sums, first):
        return dot(sums[first : first + 5, :] + sums[first + 1 : first + 6, :], spread_ref[...], high) / float(PATCH * PATCH)

    own_energy = [energy(own_sums, 5), energy(own_sums, 0)]

    def finish(part):
        scale = float(PATCH) ** 3 * jnp.sqrt((own_energy[part] + 1e-05) * (energy(other_sums.at[part], 0) + 1e-05))
        lane5 = lax.broadcasted_iota(jnp.int32, (5, 128), 1)
        peak = jnp.zeros((5, 128), F32)
        for j in range(2 * BLOCKS):
            peak = jnp.where(lane5 == j, jnp.max(peak_rows[part, j, 0:5, :], axis=1, keepdims=True), peak)
        height = peak / scale + 1e-05
        rows = jnp.concatenate([jnp.sum(windows[part] * basis_ref[e][None], axis=1) for e in range(6)], 0)
        values = dot(rows, gather_ref[...], high)
        return [values[8 * e : 8 * e + 5] / scale / height for e in range(6)]

    wait_chunk(0)
    other_rows(0)

    def chunk(c, carry):
        wait_chunk(c)
        other_rows(c)
        patch_rows(c - 1)
        return carry

    lax.fori_loop(1, CHUNKS, chunk, 0)
    for e, value in enumerate(finish(BEFORE)):
        result[e, 0:5, :] = value
    pl.when(place.there(copies[ret][0]))(lambda: remote(ret).start())
    for e, value in enumerate(finish(AFTER)):
        out_ref[e, 0:5, 0, :] = value[:, :10]
    for n in range(len(copies)):
        if n != ret:
            pl.when(place.there(copies[n][0]))(lambda: remote(n).wait_send())
    wait_for(ret)
    for e in range(6):
        out_ref[e, 5:10, 0, :] = returned[e, 0:5, :10]
    pl.when(place.there(copies[ret][0]))(lambda: remote(ret).wait_send())


def correlate(tile, peaks):
    tables = host_tables()
    apart = pl.BlockSpec(memory_space=pltpu.HBM)
    count = 5 + 4 * CHUNKS
    return pl.pallas_call(
        kernel,
        out_shape=jax.ShapeDtypeStruct((6, 10, 1, 10), F32),
        in_specs=[apart] * (2 + len(tables)),
        out_specs=pl.BlockSpec(memory_space=pltpu.VMEM),
        scratch_shapes=[
            pltpu.VMEM((ROWS, LANES), BF16),
            pltpu.VMEM((2, PART_ROWS, MAIN), BF16),
            pltpu.VMEM((MAIN // 2, 128), BF16),
            pltpu.VMEM((ROWS // 2, 128), BF16),
            pltpu.VMEM((2, PART_ROWS // 2, 128), BF16),
            *[pltpu.VMEM(t.shape, t.dtype) for t in tables],
            pltpu.VMEM((ROWS, LANES), BF16),
            pltpu.VMEM((ROWS, LANES), BF16),
            pltpu.VMEM((2, PART_ROWS, LANES), BF16),
            pltpu.VMEM((2, PART_ROWS, LANES), BF16),
            pltpu.VMEM((10, 256, LANES), BF16),
            pltpu.VMEM((16, LANES), F32),
            pltpu.VMEM((2, 8, LANES), F32),
            pltpu.VMEM((2, 10, 144, 128), F32),
            pltpu.VMEM((2, 8, 8, 128), F32),
            pltpu.VMEM((2, 10, 8, 128), F32),
            pltpu.VMEM((6, 8, 128), F32),
            pltpu.VMEM((6, 8, 128), F32),
            pltpu.VMEM((5, 2, 10), jnp.int32),
            pltpu.SMEM((2, 5, 2, 10), jnp.int32),
            pltpu.SemaphoreType.DMA((2 + len(tables),)),
            pltpu.SemaphoreType.DMA((count,)),
            pltpu.SemaphoreType.DMA((count,)),
        ],
        compiler_params=pltpu.CompilerParams(
            collective_id=0, has_side_effects=True, vmem_limit_bytes=48 * 1024 * 1024
        ),
    )(tile, peaks, *[jnp.asarray(t) for t in tables])


def body(sections, peaks, valid):
    out = correlate(sections[0], jnp.transpose(peaks, (0, 2, 1, 3))[0])
    return jnp.transpose(out, (2, 0, 1, 3)) * valid[:, None].astype(F32)


def solution(mesh):
    in_specs = (P("gz", "gy", "gx"), P("gz", None, "gy", "gx"), P("gz", "gy", "gx"))
    out_specs = P("gz", None, "gy", "gx")
    return jax.shard_map(body, mesh=mesh, in_specs=in_specs, out_specs=out_specs, check_vma=False)
```

```python
import functools
import math

import jax
import jax.numpy as jnp
import ml_dtypes
import numpy as np
from jax import lax
from jax.experimental import pallas as pl
from jax.experimental.pallas import tpu as pltpu
from jax.sharding import PartitionSpec as P

PATCH = 128
STRIDE = 64
WIN = 5
HALF = 64
ROWS = 704
LANES = 768
BLOCKS = 5
PAIRS = 3
CHUNKS = 6
PART_ROWS = CHUNKS * STRIDE
F32 = jnp.float32
BF16 = jnp.bfloat16


def host_tables():
    index = np.arange(PATCH)
    phase = ((index[:, None] * index[None, :]) % PATCH).astype(np.float32) * np.float32(
        2.0 * math.pi / PATCH
    )
    rounded = lambda v: v.astype(ml_dtypes.bfloat16).astype(np.float32)
    cosine, sine = rounded(np.cos(phase)), rounded(np.sin(phase))
    first = np.zeros((256, 256), np.float32)
    last = np.zeros((256, 256), np.float32)
    weight = np.where(np.arange(HALF) == 0, 1.0, 2.0).astype(np.float32)
    for w in range(2):
        rows = slice(64 * w, 64 * w + 128)
        real, imag = slice(64 * w, 64 * w + 64), slice(128 + 64 * w, 192 + 64 * w)
        lags = slice(128 * w, 128 * w + 128)
        first[rows, real] = cosine[:HALF].T
        first[rows, imag] = -sine[:HALF].T
        first[rows, 128 + 64 * w] = 0.0
        last[real, lags] = (cosine[:, :HALF] * weight).T
        last[imag, lags] = (-sine[:, :HALF] * weight).T
        last[128 + 64 * w, lags] = cosine[:, HALF]
    nyquist = np.zeros((LANES, 128), np.float32)
    for b in range(BLOCKS):
        for w in range(2):
            start = 128 * b + 64 * w
            nyquist[start : start + 128, b + 64 * w] = cosine[HALF]
    forward = np.block([[cosine, sine], [-sine, cosine]])
    inverse = np.stack([np.block([[cosine, sine], [sine, -cosine]]), np.block([[cosine, -sine], [sine, cosine]])])
    offsets = np.arange(WIN, dtype=np.float32) - WIN // 2
    ones = np.ones(WIN, np.float32)
    square = offsets * offsets - np.mean(offsets * offsets)
    pairs = [(ones, ones), (offsets, ones), (ones, offsets), (square, ones), (ones, square), (offsets, offsets)]
    basis = np.zeros((6, 8, 128), np.float32)
    for e, (p, q) in enumerate(pairs):
        func = p[:, None] * q[None, :]
        func = func / np.sqrt(np.sum(func * func))
        for j in range(2 * BLOCKS):
            basis[e, :WIN, 8 * j : 8 * j + WIN] = func
    gather = np.zeros((128, 128), np.float32)
    for j in range(2 * BLOCKS):
        gather[8 * j : 8 * j + 8, j] = 1.0
    spread = np.zeros((LANES, 128), np.float32)
    for j in range(2 * BLOCKS):
        spread[64 * j : 64 * j + 128, j] = 1.0
    low = lambda v: v.astype(ml_dtypes.bfloat16)
    return low(first), low(nyquist), low(forward), low(inverse), low(last), basis, gather, spread


def dot(a, b, precision=None):
    return lax.dot_general(a, b, (((1,), (0,)), ((), ())), precision=precision, preferred_element_type=F32)


def row_transform(x, first_ref, block):
    return dot(x[:, 128 * block : 128 * block + 256], first_ref[...]).astype(BF16)


def unpack(packed):
    wide = packed.astype(F32)
    return jnp.concatenate([wide, pltpu.roll(wide, HALF, 1)], 0).astype(BF16)


def square_sums(x, sums_ref, strip):
    x = x.astype(F32)
    sums_ref[pl.ds(strip, 1), :] = jnp.sum(x * x, axis=0, keepdims=True)


def column_transform(real_ref, imag_ref, start, forward_ref):
    data = jnp.concatenate([real_ref[pl.ds(start, 128), :], imag_ref[pl.ds(start, 128), :]], 0)
    return dot(forward_ref[...], data).astype(BF16)


MAIN = 640
BEFORE, AFTER = 0, 1


class Place:
    def __init__(self):
        self.at = {name: lax.axis_index(name) for name in ("gz", "gx", "gy")}
        self.size = {name: lax.axis_size(name) for name in ("gz", "gx", "gy")}

    def there(self, step):
        inside = None
        for name, move in zip(("gz", "gx", "gy"), step):
            if move:
                ok = self.at[name] + move < self.size[name] if move > 0 else self.at[name] + move >= 0
                inside = ok if inside is None else jnp.logical_and(inside, ok)
        return inside

    def device(self, step):
        return {name: self.at[name] + move for name, move in zip(("gz", "gx", "gy"), step)}


def back(step):
    return tuple(-move for move in step)


def kernel(tile_ref, peaks_ref, first_hbm, nyquist_hbm, forward_hbm, inverse_hbm, last_hbm, basis_hbm, gather_hbm, spread_hbm,
           out_ref,
           own, other, packed, own_edge, other_edge,
           first_ref, nyquist_ref, forward_ref, inverse_ref, last_ref, basis_ref, gather_ref, spread_ref,
           own_re, own_im, other_re, other_im, spectra, own_sums, other_sums, surface, windows, peak_rows,
           result, returned, far_peaks, peaks, local_sems, send_sems, recv_sems):
    place = Place()
    tables = [(first_hbm, first_ref), (nyquist_hbm, nyquist_ref), (forward_hbm, forward_ref), (inverse_hbm, inverse_ref),
              (last_hbm, last_ref), (basis_hbm, basis_ref), (gather_hbm, gather_ref), (spread_hbm, spread_ref)]
    main = pl.ds(0, MAIN)
    tile_copy = pltpu.make_async_copy(tile_ref, own.at[main, main], local_sems.at[0])
    local = [pltpu.make_async_copy(peaks_ref.at[pl.ds(0, 5)], peaks.at[AFTER], local_sems.at[1])]
    local += [pltpu.make_async_copy(a, b, local_sems.at[2 + n]) for n, (a, b) in enumerate(tables)]
    tile_copy.start()
    for copy in local:
        copy.start()

    copies = [
        ((0, 0, -1), tile_ref.at[pl.ds(0, STRIDE), :], own.at[pl.ds(MAIN, STRIDE), main]),
        ((0, -1, 0), packed, own_edge.at[pl.ds(0, MAIN // 2)]),
        ((0, -1, -1), packed.at[pl.ds(0, 32)], own_edge.at[pl.ds(MAIN // 2, 32)]),
        ((1, 0, 0), peaks_ref.at[pl.ds(5, 5)], far_peaks),
        ((-1, 0, 0), result, returned),
    ]
    ret = len(copies) - 1
    base = len(copies)
    for c in range(CHUNKS):
        for part in (BEFORE, AFTER):
            move = -1 if part == AFTER else 1
            strip = c if part == AFTER else (5 + c) % 10
            low = -1 if part == BEFORE and c == CHUNKS - 1 else 0
            rows = pl.ds(STRIDE * c, STRIDE)
            copies.append(((move, 0, low), tile_ref.at[pl.ds(STRIDE * strip, STRIDE), :], other.at[part, rows, :]))
            copies.append(((move, -1, low), packed.at[pl.ds(32 * strip, 32)], other_edge.at[part, pl.ds(32 * c, 32)]))

    def remote(n):
        step, source, destination = copies[n]
        return pltpu.make_async_remote_copy(
            src_ref=source, dst_ref=destination, send_sem=send_sems.at[n], recv_sem=recv_sems.at[n],
            device_id=place.device(step), device_id_type=pl.DeviceIdType.MESH,
        )

    def wait_for(n):
        pl.when(place.there(back(copies[n][0])))(lambda: remote(n).wait_recv())

    @pl.when(place.at["gy"] == place.size["gy"] - 1)
    def _():
        own[MAIN:ROWS, :MAIN] = jnp.zeros((STRIDE, MAIN), BF16)
        own_edge[MAIN // 2 :, :] = jnp.zeros((32, 128), BF16)
        other[BEFORE, PART_ROWS - STRIDE :, :] = jnp.zeros((STRIDE, MAIN), BF16)
        other_edge[BEFORE, PART_ROWS // 2 - 32 :, :] = jnp.zeros((32, 128), BF16)

    @pl.when(place.at["gx"] == place.size["gx"] - 1)
    def _():
        own_edge[...] = jnp.zeros_like(own_edge)
        other_edge[...] = jnp.zeros_like(other_edge)

    @pl.when(place.at["gz"] == place.size["gz"] - 1)
    def _():
        other[AFTER] = jnp.zeros((PART_ROWS, MAIN), BF16)
        other_edge[AFTER] = jnp.zeros((PART_ROWS // 2, 128), BF16)
        returned[...] = jnp.zeros_like(returned)

    @pl.when(place.at["gz"] == 0)
    def _():
        other[BEFORE] = jnp.zeros((PART_ROWS, MAIN), BF16)
        other_edge[BEFORE] = jnp.zeros((PART_ROWS // 2, 128), BF16)
        far_peaks[...] = jnp.zeros_like(far_peaks)

    lane = lax.broadcasted_iota(jnp.int32, (128, 128), 1)
    slot = lax.rem(lane, HALF) == 0
    lane8 = lax.broadcasted_iota(jnp.int32, (8, 128), 1) // 8
    left = lax.broadcasted_iota(jnp.int32, (32, 128), 1) < HALF

    barrier = pltpu.get_barrier_semaphore()
    steps = sorted({step for step, _, _ in copies})
    for step in steps:
        @pl.when(place.there(back(step)))
        def _():
            pl.semaphore_signal(barrier, inc=1, device_id=place.device(back(step)), device_id_type=pl.DeviceIdType.MESH)
    tile_copy.wait()
    for n in range(MAIN // STRIDE):
        block = own[STRIDE * n : STRIDE * n + STRIDE, 0:128].astype(F32)
        packed[32 * n : 32 * n + 32, :] = jnp.where(left, block[:32], pltpu.roll(block[32:], HALF, 1)).astype(BF16)
    pl.semaphore_wait(barrier, sum(place.there(step).astype(jnp.int32) for step in steps))
    for n in range(len(copies)):
        if n != ret:
            pl.when(place.there(copies[n][0]))(lambda: remote(n).start())

    windows[...] = jnp.zeros_like(windows)
    peak_rows[...] = jnp.zeros_like(peak_rows)
    for copy in local:
        copy.wait()

    def keep(re, im, rows, b, out):
        re[rows, 128 * b : 128 * b + 128] = out[:, :128]
        im[rows, 128 * b : 128 * b + 128] = out[:, 128:]

    def keep_nyquist(re, im, rows, out):
        re[rows, 128 * BLOCKS :] = out
        im[rows, 128 * BLOCKS :] = jnp.zeros((out.shape[0], 128), BF16)

    for b in range(BLOCKS - 1):
        keep(own_re, own_im, slice(0, MAIN), b, row_transform(own[0:MAIN, :], first_ref, b))
    for n in range(3):
        wait_for(n)

    def own_strip(strip, carry):
        rows = pl.ds(pl.multiple_of(strip * STRIDE, STRIDE), STRIDE)
        own[rows, MAIN:] = unpack(own_edge[pl.ds(pl.multiple_of(strip * 32, 32), 32), :])
        square_sums(own[rows, :], own_sums, strip)
        return carry

    lax.fori_loop(0, ROWS // STRIDE, own_strip, 0)
    for b in range(BLOCKS - 1):
        keep(own_re, own_im, slice(MAIN, ROWS), b, row_transform(own[MAIN:ROWS, :], first_ref, b))
    keep(own_re, own_im, slice(0, ROWS), BLOCKS - 1, row_transform(own[...], first_ref, BLOCKS - 1))
    keep_nyquist(own_re, own_im, slice(0, ROWS), dot(own[...], nyquist_ref[...]).astype(BF16))

    def own_spectra(i, carry):
        for half in range(2):
            row = 5 * half + i
            spectra[row] = column_transform(own_re, own_im, pl.multiple_of(row * STRIDE, STRIDE), forward_ref)
        return carry

    lax.fori_loop(0, 5, own_spectra, 0)
    wait_for(3)
    far = pltpu.make_async_copy(far_peaks, peaks.at[BEFORE], local_sems.at[1])
    far.start()
    far.wait()

    both = (BEFORE, AFTER)

    def wait_chunk(c):
        rows = pl.ds(pl.multiple_of(c * STRIDE, STRIDE), STRIDE)
        half = pl.ds(pl.multiple_of(c * 32, 32), 32)
        for part in both:
            there = place.there((1, 0, 0)) if part == AFTER else jnp.logical_and(
                place.there((-1, 0, 0)), jnp.logical_or(c < CHUNKS - 1, place.there((0, 0, 1))))
            beside = jnp.logical_and(there, place.there((0, 1, 0)))
            n = base + 4 * c + 2 * part
            for k, (ok, ref) in enumerate(((there, other.at[part, rows, :]), (beside, other_edge.at[part, half]))):
                @pl.when(ok)
                def _():
                    pltpu.make_async_remote_copy(
                        src_ref=ref, dst_ref=ref, send_sem=send_sems.at[n + k], recv_sem=recv_sems.at[n + k],
                        device_id=place.device((0, 0, 0)), device_id_type=pl.DeviceIdType.MESH,
                    ).wait_recv()

    def other_rows(c):
        rows = pl.ds(pl.multiple_of(c * STRIDE, STRIDE), STRIDE)
        half = pl.ds(pl.multiple_of(c * 32, 32), 32)
        pieces = [jnp.concatenate([other[part, rows, :], unpack(other_edge[part, half, :])], 1) for part in both]
        x = jnp.concatenate(pieces, 0)
        for b in range(BLOCKS):
            out = row_transform(x, first_ref, b)
            for part in both:
                keep(other_re.at[part], other_im.at[part], rows, b, out[64 * part : 64 * part + 64])
        out = dot(x, nyquist_ref[...]).astype(BF16)
        for part in both:
            keep_nyquist(other_re.at[part], other_im.at[part], rows, out[64 * part : 64 * part + 64])
            square_sums(pieces[part], other_sums.at[part], c)

    def patch_rows(i):
        start = pl.multiple_of(i * STRIDE, STRIDE)
        crosses = []
        for part in both:
            a = spectra[(5 if part == BEFORE else 0) + i].astype(F32)
            b = column_transform(other_re.at[part], other_im.at[part], start, forward_ref).astype(F32)
            ar, ai, br, bi = a[:128], a[128:], b[:128], b[128:]
            crosses.append(jnp.concatenate([(ar * br + ai * bi).astype(BF16), (ar * bi - ai * br).astype(BF16)], 0))
        for part in both:
            turned = dot(inverse_ref[part], crosses[part])
            extra = turned[:128, 128 * BLOCKS :]
            for b in range(BLOCKS):
                lanes = slice(128 * b, 128 * b + 128)
                moved = extra if b == 0 else pltpu.roll(extra, 128 - b, 1)
                imag = jnp.where(slot, moved, turned[128:, lanes]).astype(BF16)
                out = dot(jnp.concatenate([turned[:128, lanes].astype(BF16), imag], 1), last_ref[...])
                for w in range(2):
                    piece = out[:, 128 * w : 128 * w + 128]
                    j = 2 * b + w
                    surface[part, j, 8:136, :] = piece
                    surface[part, j, 0:8, :] = piece[120:]
                    surface[part, j, 136:144, :] = piece[:8]
                    peak_rows[part, j, pl.ds(i, 1), :] = jnp.max(jnp.abs(piece), axis=0, keepdims=True)
        for part in both:
            held = jnp.zeros((8, 128), F32)
            for j in range(2 * BLOCKS):
                dy = peaks[part, i, 0, j]
                dx = peaks[part, i, 1, j]
                piece = surface[part, j, pl.ds(dy + 6, 8), :]
                shift = lax.rem(8 * j + 2 + 128 - dx, 128)
                held = jnp.where(lane8 == j, pltpu.roll(piece, shift, 1), held)
            windows[part, i] = held

    high = lax.Precision.HIGHEST

    def energy(sums, first):
        return dot(sums[first : first + 5, :] + sums[first + 1 : first + 6, :], spread_ref[...], high) / float(PATCH * PATCH)

    own_energy = [energy(own_sums, 5), energy(own_sums, 0)]

    def finish(part):
        scale = float(PATCH) ** 3 * jnp.sqrt((own_energy[part] + 1e-05) * (energy(other_sums.at[part], 0) + 1e-05))
        lane5 = lax.broadcasted_iota(jnp.int32, (5, 128), 1)
        peak = jnp.zeros((5, 128), F32)
        for j in range(2 * BLOCKS):
            peak = jnp.where(lane5 == j, jnp.max(peak_rows[part, j, 0:5, :], axis=1, keepdims=True), peak)
        height = peak / scale + 1e-05
        rows = jnp.concatenate([jnp.sum(windows[part] * basis_ref[e][None], axis=1) for e in range(6)], 0)
        values = dot(rows, gather_ref[...], high)
        return [values[8 * e : 8 * e + 5] / scale / height for e in range(6)]

    wait_chunk(0)
    other_rows(0)

    def chunk(c, carry):
        wait_chunk(c)
        other_rows(c)
        patch_rows(c - 1)
        return carry

    lax.fori_loop(1, CHUNKS, chunk, 0)
    for e, value in enumerate(finish(BEFORE)):
        result[e, 0:5, :] = value
    pl.when(place.there(copies[ret][0]))(lambda: remote(ret).start())
    for e, value in enumerate(finish(AFTER)):
        out_ref[e, 0:5, 0, :] = value[:, :10]
    for n in range(len(copies)):
        if n != ret:
            pl.when(place.there(copies[n][0]))(lambda: remote(n).wait_send())
    wait_for(ret)
    for e in range(6):
        out_ref[e, 5:10, 0, :] = returned[e, 0:5, :10]
    pl.when(place.there(copies[ret][0]))(lambda: remote(ret).wait_send())


def correlate(tile, peaks):
    tables = host_tables()
    apart = pl.BlockSpec(memory_space=pltpu.HBM)
    count = 5 + 4 * CHUNKS
    return pl.pallas_call(
        kernel,
        out_shape=jax.ShapeDtypeStruct((6, 10, 1, 10), F32),
        in_specs=[apart] * (2 + len(tables)),
        out_specs=pl.BlockSpec(memory_space=pltpu.VMEM),
        scratch_shapes=[
            pltpu.VMEM((ROWS, LANES), BF16),
            pltpu.VMEM((2, PART_ROWS, MAIN), BF16),
            pltpu.VMEM((MAIN // 2, 128), BF16),
            pltpu.VMEM((ROWS // 2, 128), BF16),
            pltpu.VMEM((2, PART_ROWS // 2, 128), BF16),
            *[pltpu.VMEM(t.shape, t.dtype) for t in tables],
            pltpu.VMEM((ROWS, LANES), BF16),
            pltpu.VMEM((ROWS, LANES), BF16),
            pltpu.VMEM((2, PART_ROWS, LANES), BF16),
            pltpu.VMEM((2, PART_ROWS, LANES), BF16),
            pltpu.VMEM((10, 256, LANES), BF16),
            pltpu.VMEM((16, LANES), F32),
            pltpu.VMEM((2, 8, LANES), F32),
            pltpu.VMEM((2, 10, 144, 128), F32),
            pltpu.VMEM((2, 8, 8, 128), F32),
            pltpu.VMEM((2, 10, 8, 128), F32),
            pltpu.VMEM((6, 8, 128), F32),
            pltpu.VMEM((6, 8, 128), F32),
            pltpu.VMEM((5, 2, 10), jnp.int32),
            pltpu.SMEM((2, 5, 2, 10), jnp.int32),
            pltpu.SemaphoreType.DMA((2 + len(tables),)),
            pltpu.SemaphoreType.DMA((count,)),
            pltpu.SemaphoreType.DMA((count,)),
        ],
        compiler_params=pltpu.CompilerParams(
            collective_id=0, has_side_effects=True, vmem_limit_bytes=62 * 1024 * 1024
        ),
    )(tile, peaks, *[jnp.asarray(t) for t in tables])


def body(sections, peaks, valid):
    out = correlate(sections[0], jnp.transpose(peaks, (0, 2, 1, 3))[0])
    return jnp.transpose(out, (2, 0, 1, 3)) * valid[:, None].astype(F32)


def solution(mesh):
    in_specs = (P("gz", "gy", "gx"), P("gz", None, "gy", "gx"), P("gz", "gy", "gx"))
    out_specs = P("gz", None, "gy", "gx")
    return jax.shard_map(body, mesh=mesh, in_specs=in_specs, out_specs=out_specs, check_vma=False)
```

```python
import functools
import math

import jax
import jax.numpy as jnp
import ml_dtypes
import numpy as np
from jax import lax
from jax.experimental import pallas as pl
from jax.experimental.pallas import tpu as pltpu
from jax.sharding import PartitionSpec as P

PATCH = 128
STRIDE = 64
WIN = 5
HALF = 64
ROWS = 704
LANES = 768
BLOCKS = 5
STEPS = 5
F32 = jnp.float32
BF16 = jnp.bfloat16


def host_tables():
    index = np.arange(PATCH)
    phase = ((index[:, None] * index[None, :]) % PATCH).astype(np.float32) * np.float32(
        2.0 * math.pi / PATCH
    )
    rounded = lambda v: v.astype(ml_dtypes.bfloat16).astype(np.float32)
    cosine, sine = rounded(np.cos(phase)), rounded(np.sin(phase))
    first = np.zeros((256, 256), np.float32)
    last = np.zeros((256, 256), np.float32)
    weight = np.where(np.arange(HALF) == 0, 1.0, 2.0).astype(np.float32)
    for w in range(2):
        rows = slice(64 * w, 64 * w + 128)
        real, imag = slice(64 * w, 64 * w + 64), slice(128 + 64 * w, 192 + 64 * w)
        lags = slice(128 * w, 128 * w + 128)
        first[rows, real] = cosine[:HALF].T
        first[rows, imag] = -sine[:HALF].T
        first[rows, 128 + 64 * w] = 0.0
        last[real, lags] = (cosine[:, :HALF] * weight).T
        last[imag, lags] = (-sine[:, :HALF] * weight).T
        last[128 + 64 * w, lags] = cosine[:, HALF]
    nyquist = np.zeros((LANES, 128), np.float32)
    for b in range(BLOCKS):
        for w in range(2):
            start = 128 * b + 64 * w
            nyquist[start : start + 128, b + 64 * w] = cosine[HALF]
    forward = np.block([[cosine, sine], [-sine, cosine]])
    inverse = np.stack([np.block([[cosine, sine], [sine, -cosine]]), np.block([[cosine, -sine], [sine, cosine]])])
    offsets = np.arange(WIN, dtype=np.float32) - WIN // 2
    ones = np.ones(WIN, np.float32)
    square = offsets * offsets - np.mean(offsets * offsets)
    pairs = [(ones, ones), (offsets, ones), (ones, offsets), (square, ones), (ones, square), (offsets, offsets)]
    basis = np.zeros((6, 8, 128), np.float32)
    for e, (p, q) in enumerate(pairs):
        func = p[:, None] * q[None, :]
        func = func / np.sqrt(np.sum(func * func))
        for j in range(2 * BLOCKS):
            basis[e, :WIN, 8 * j : 8 * j + WIN] = func
    gather = np.zeros((128, 128), np.float32)
    for j in range(2 * BLOCKS):
        gather[8 * j : 8 * j + 8, j] = 1.0
    spread = np.zeros((LANES, 128), np.float32)
    for j in range(2 * BLOCKS):
        for e in range(6):
            spread[64 * j : 64 * j + 128, 16 * e + j] = 1.0
    low = lambda v: v.astype(ml_dtypes.bfloat16)
    return low(first), low(nyquist), low(forward), low(inverse), low(last), basis, gather, spread


def dot(a, b, precision=None):
    return lax.dot_general(a, b, (((1,), (0,)), ((), ())), precision=precision, preferred_element_type=F32)


def row_transform(x, first_ref, block):
    return dot(x[:, 128 * block : 128 * block + 256], first_ref[...]).astype(BF16)


def unpack(packed):
    wide = packed.astype(F32)
    return jnp.concatenate([wide, pltpu.roll(wide, HALF, 1)], 0).astype(BF16)


def square_sums(x, sums_ref, strip):
    x = x.astype(F32)
    sums_ref[pl.ds(strip, 1), :] = jnp.sum(x * x, axis=0, keepdims=True)


def column_transform(real_ref, imag_ref, start, forward_ref):
    data = jnp.concatenate([real_ref[pl.ds(start, 128), :], imag_ref[pl.ds(start, 128), :]], 0)
    return dot(forward_ref[...], data).astype(BF16)


MAIN = 640


class Place:
    def __init__(self):
        self.at = {name: lax.axis_index(name) for name in ("gz", "gx", "gy")}
        self.size = {name: lax.axis_size(name) for name in ("gz", "gx", "gy")}

    def there(self, step):
        inside = None
        for name, move in zip(("gz", "gx", "gy"), step):
            if not (isinstance(move, int) and move == 0):
                to = self.at[name] + move
                ok = jnp.logical_and(to >= 0, to < self.size[name])
                inside = ok if inside is None else jnp.logical_and(inside, ok)
        return inside

    def device(self, step):
        return {name: self.at[name] + move for name, move in zip(("gz", "gx", "gy"), step)}


def kernel(tile_ref, peaks_ref, valid_hbm, first_hbm, nyquist_hbm, forward_hbm, inverse_hbm, last_hbm, basis_hbm, gather_hbm,
           spread_hbm, out_ref,
           own, other, packed, own_edge, other_edge,
           first_ref, nyquist_ref, forward_ref, inverse_ref, last_ref, basis_ref, gather_ref, spread_ref,
           own_re, own_im, other_re, other_im, spectra, own_sums, other_sums, surface, windows, peak_rows,
           result, returned, far_peaks, valid, peaks, local_sems, send_sems, recv_sems):
    place = Place()
    second = 1 - lax.rem(place.at["gx"], 2)
    is_second = second == 1
    ahead = 2 * second - 1
    tables = [(first_hbm, first_ref), (nyquist_hbm, nyquist_ref), (forward_hbm, forward_ref), (inverse_hbm, inverse_ref),
              (last_hbm, last_ref), (basis_hbm, basis_ref), (gather_hbm, gather_ref), (spread_hbm, spread_ref)]
    main = pl.ds(0, MAIN)
    tile_copy = pltpu.make_async_copy(tile_ref, own.at[main, main], local_sems.at[0])
    local_peaks = pltpu.make_async_copy(peaks_ref, peaks, local_sems.at[1])
    tables.append((valid_hbm, valid))
    local = [pltpu.make_async_copy(a, b, local_sems.at[2 + n]) for n, (a, b) in enumerate(tables)]

    pair = place.there((-ahead, 0, 0))
    beside = place.there((0, 1, 0))
    top = pl.ds(0, STRIDE)
    low = pl.ds(MAIN, STRIDE)
    first32, last32 = pl.ds(0, 32), pl.ds(MAIN // 2, 32)
    copies = [
        ((0, 0, -1), (0, 0, 1), tile_ref.at[top, :], own.at[low, main], None),
        ((0, -1, 0), (0, 1, 0), packed, own_edge.at[pl.ds(0, MAIN // 2)], None),
        ((0, 0, -1), (0, 0, 1), own_edge.at[first32], own_edge.at[last32], beside),
        ((ahead, 0, 0), (-ahead, 0, 0), peaks_ref, far_peaks, is_second),
        ((-ahead, 0, 0), (ahead, 0, 0), result, returned, is_second),
        ((-ahead, -1, 0), (-ahead, 1, 0), packed.at[pl.ds(0, 96)], other_edge.at[pl.ds(0, 96)], None),
        ((-ahead, -1, 0), (-ahead, 1, 0), packed.at[pl.ds(96, 224)], other_edge.at[pl.ds(96, 224)], None),
        ((0, 0, -1), (0, 0, 1), other_edge.at[first32], other_edge.at[last32], jnp.logical_and(pair, beside)),
        ((0, 0, -1), (0, 0, 1), other.at[top, main], other.at[low, main], pair),
    ]
    FAR, RETURN, EDGE, LATER_EDGE, CORNER, FORWARD = 3, 4, 5, 6, 7, 8
    base = len(copies)
    for start, count in [(0, 64)] + [(64 + 128 * t, 128) for t in range(STEPS - 1)] + [(576, 64)]:
        rows = pl.ds(start, count)
        copies.append(((ahead, 0, 0), (-ahead, 0, 0), tile_ref.at[rows, :], other.at[rows, main], None))

    def remote(n):
        step, _, source, destination, _ = copies[n]
        return pltpu.make_async_remote_copy(
            src_ref=source, dst_ref=destination, send_sem=send_sems.at[n], recv_sem=recv_sems.at[n],
            device_id=place.device(step), device_id_type=pl.DeviceIdType.MESH,
        )

    def when(n, side):
        ok = place.there(copies[n][side])
        return ok if copies[n][4] is None else jnp.logical_and(ok, copies[n][4])

    def send(n):
        pl.when(when(n, 0))(lambda: remote(n).start())

    def sent(n):
        pl.when(when(n, 0))(lambda: remote(n).wait_send())

    def wait_for(n):
        pl.when(when(n, 1))(lambda: remote(n).wait_recv())

    @pl.when(place.at["gy"] == place.size["gy"] - 1)
    def _():
        own[MAIN:ROWS, :MAIN] = jnp.zeros((STRIDE, MAIN), BF16)
        own_edge[MAIN // 2 :, :] = jnp.zeros((32, 128), BF16)
        other[MAIN:ROWS, :MAIN] = jnp.zeros((STRIDE, MAIN), BF16)
        other_edge[MAIN // 2 :, :] = jnp.zeros((32, 128), BF16)

    @pl.when(place.at["gx"] == place.size["gx"] - 1)
    def _():
        own_edge[...] = jnp.zeros_like(own_edge)
        other_edge[...] = jnp.zeros_like(other_edge)

    @pl.when(jnp.logical_not(pair))
    def _():
        other[:, :MAIN] = jnp.zeros((ROWS, MAIN), BF16)
        other_edge[...] = jnp.zeros_like(other_edge)
        far_peaks[...] = jnp.zeros_like(far_peaks)

    @pl.when(place.at["gz"] == place.size["gz"] - 1)
    def _():
        returned[...] = jnp.zeros_like(returned)

    barrier = pltpu.get_barrier_semaphore()
    meetings = [((0, 0, -1), (0, 0, 1)), ((0, -1, 0), (0, 1, 0)), ((ahead, 0, 0), (-ahead, 0, 0)),
                ((-ahead, 0, 0), (ahead, 0, 0)), ((-ahead, -1, 0), (-ahead, 1, 0))]
    for _, step in meetings:
        @pl.when(place.there(step))
        def _():
            pl.semaphore_signal(barrier, inc=1, device_id=place.device(step), device_id_type=pl.DeviceIdType.MESH)
    tile_copy.start()
    for copy in local:
        copy.start()
    pl.when(jnp.logical_not(is_second))(lambda: local_peaks.start())
    left = lax.broadcasted_iota(jnp.int32, (32, 128), 1) < HALF
    tile_copy.wait()
    for n in range(MAIN // STRIDE):
        block = own[STRIDE * n : STRIDE * n + STRIDE, 0:128].astype(F32)
        packed[32 * n : 32 * n + 32, :] = jnp.where(left, block[:32], pltpu.roll(block[32:], HALF, 1)).astype(BF16)
    pl.semaphore_wait(barrier, sum(place.there(step).astype(jnp.int32) for step, _ in meetings))
    for n in (1, EDGE, 0, base, FAR, LATER_EDGE, *range(base + 1, len(copies))):
        send(n)

    windows[...] = jnp.zeros_like(windows)
    peak_rows[...] = jnp.zeros_like(peak_rows)
    for copy in local:
        copy.wait()

    def keep(re, im, rows, b, out):
        re[rows, 128 * b : 128 * b + 128] = out[:, :128]
        im[rows, 128 * b : 128 * b + 128] = out[:, 128:]

    def keep_nyquist(re, im, rows, out):
        re[rows, 128 * BLOCKS :] = out
        im[rows, 128 * BLOCKS :] = jnp.zeros((out.shape[0], 128), BF16)

    for b in range(BLOCKS - 1):
        keep(own_re, own_im, slice(0, MAIN), b, row_transform(own[0:MAIN, :], first_ref, b))
    wait_for(1)
    send(2)
    wait_for(base)
    send(FORWARD)
    wait_for(EDGE)
    send(CORNER)
    wait_for(0)
    wait_for(2)

    def own_strip(strip, carry):
        rows = pl.ds(pl.multiple_of(strip * STRIDE, STRIDE), STRIDE)
        own[rows, MAIN:] = unpack(own_edge[pl.ds(pl.multiple_of(strip * 32, 32), 32), :])
        square_sums(own[rows, :], own_sums, strip)
        return carry

    lax.fori_loop(0, ROWS // STRIDE, own_strip, 0)
    for b in range(BLOCKS - 1):
        keep(own_re, own_im, slice(MAIN, ROWS), b, row_transform(own[MAIN:ROWS, :], first_ref, b))
    keep(own_re, own_im, slice(0, ROWS), BLOCKS - 1, row_transform(own[...], first_ref, BLOCKS - 1))
    keep_nyquist(own_re, own_im, slice(0, ROWS), dot(own[...], nyquist_ref[...]).astype(BF16))

    def own_spectra(i, carry):
        for row in (2 * i, 2 * i + 1):
            spectra[row] = column_transform(own_re, own_im, pl.multiple_of(row * STRIDE, STRIDE), forward_ref)
        return carry

    lax.fori_loop(0, 5, own_spectra, 0)
    wait_for(FAR)
    far = pltpu.make_async_copy(far_peaks, peaks, local_sems.at[1])
    pl.when(is_second)(lambda: far.start())
    pl.when(is_second)(lambda: far.wait())
    pl.when(jnp.logical_not(is_second))(lambda: local_peaks.wait())

    lane = lax.broadcasted_iota(jnp.int32, (128, 128), 1)
    slot = lax.rem(lane, HALF) == 0
    lane8 = lax.broadcasted_iota(jnp.int32, (8, 128), 1) // 8

    def other_rows(start, count):
        rows = pl.ds(pl.multiple_of(start, STRIDE), count)
        for k in range(count // STRIDE):
            strip = lax.div(start, STRIDE) + k
            here = pl.ds(pl.multiple_of(strip * STRIDE, STRIDE), STRIDE)
            edge = unpack(other_edge[pl.ds(pl.multiple_of(strip * 32, 32), 32), :])
            other[here, MAIN:] = edge
            square_sums(jnp.concatenate([other[here, :MAIN], edge], 1), other_sums, strip)
        x = other[rows, :]
        for b in range(BLOCKS):
            keep(other_re, other_im, rows, b, row_transform(x, first_ref, b))
        keep_nyquist(other_re, other_im, rows, dot(x, nyquist_ref[...]).astype(BF16))

    def patch_rows(rows):
        crosses = []
        for i in rows:
            a = spectra[i].astype(F32)
            b = column_transform(other_re, other_im, pl.multiple_of(i * STRIDE, STRIDE), forward_ref).astype(F32)
            ar, ai, br, bi = a[:128], a[128:], b[:128], b[128:]
            crosses.append(jnp.concatenate([(ar * br + ai * bi).astype(BF16), (ar * bi - ai * br).astype(BF16)], 0))
        for k, i in enumerate(rows):
            turned = dot(inverse_ref[1 - second], crosses[k])
            extra = turned[:128, 128 * BLOCKS :]
            for b in range(BLOCKS):
                lanes = slice(128 * b, 128 * b + 128)
                moved = extra if b == 0 else pltpu.roll(extra, 128 - b, 1)
                imag = jnp.where(slot, moved, turned[128:, lanes]).astype(BF16)
                out = dot(jnp.concatenate([turned[:128, lanes].astype(BF16), imag], 1), last_ref[...])
                for w in range(2):
                    piece = out[:, 128 * w : 128 * w + 128]
                    j = 2 * b + w
                    surface[k, j, 8:136, :] = piece
                    surface[k, j, 0:8, :] = piece[120:]
                    surface[k, j, 136:144, :] = piece[:8]
                    peak_rows[j, pl.ds(i, 1), :] = jnp.max(jnp.abs(piece), axis=0, keepdims=True)
        for k, i in enumerate(rows):
            held = jnp.zeros((8, 128), F32)
            for j in range(2 * BLOCKS):
                dy = peaks[i, 0, j]
                dx = peaks[i, 1, j]
                piece = surface[k, j, pl.ds(dy + 6, 8), :]
                shift = lax.rem(8 * j + 2 + 128 - dx, 128)
                held = jnp.where(lane8 == j, pltpu.roll(piece, shift, 1), held)
            windows[i] = held

    high = lax.Precision.HIGHEST

    def energy(sums):
        return dot(sums[0:10, :] + sums[1:11, :], spread_ref[...], high) / float(PATCH * PATCH)

    own_energy = energy(own_sums)
    other_rows(jnp.int32(0), STRIDE)

    def step(t, carry):
        start = pl.multiple_of(128 * t + 64, 64)
        rows = other.at[pl.ds(start, 128), main]

        pl.when(t == 1)(lambda: wait_for(LATER_EDGE))

        @pl.when(pair)
        def _():
            pltpu.make_async_remote_copy(
                src_ref=rows, dst_ref=rows, send_sem=send_sems.at[base + 1 + t], recv_sem=recv_sems.at[base + 1 + t],
                device_id=place.device((0, 0, 0)), device_id_type=pl.DeviceIdType.MESH,
            ).wait_recv()

        other_rows(start, 128)
        patch_rows((2 * t, 2 * t + 1))
        return carry

    lax.fori_loop(0, STEPS - 1, step, 0)
    wait_for(base + STEPS)
    wait_for(FORWARD)
    wait_for(CORNER)
    other_rows(jnp.int32(576), 128)
    scale = float(PATCH) ** 3 * jnp.sqrt((own_energy + 1e-05) * (energy(other_sums) + 1e-05))
    patch_rows((8, 9))

    group = lax.rem(lax.broadcasted_iota(jnp.int32, (10, 128), 1), 16)
    peak = jnp.zeros((10, 128), F32)
    for j in range(2 * BLOCKS):
        peak = jnp.where(group == j, jnp.max(peak_rows[j, 0:10, :], axis=1, keepdims=True), peak)
    height = peak / scale + 1e-05
    sums = jnp.concatenate([jnp.sum(windows[...] * basis_ref[e][None], axis=1) for e in range(6)], 0)
    values = dot(sums, gather_ref[...], high)
    joined = values[0:16]
    for e in range(1, 6):
        joined = joined + pltpu.roll(values[16 * e : 16 * e + 16], 16 * e, 1)
    result[0:10, :] = joined[0:10] / scale / height
    send(RETURN)

    def give(coefficients):
        for e in range(6):
            moved = coefficients if e == 0 else pltpu.roll(coefficients, 128 - 16 * e, 1)
            out_ref[e, :, 0, :] = moved[0:10, :10] * valid[:, 0, :].astype(F32)

    for n in range(len(copies)):
        if n != RETURN:
            sent(n)

    @pl.when(jnp.logical_not(is_second))
    def _():
        give(result[...])

    @pl.when(is_second)
    def _():
        wait_for(RETURN)
        give(returned[...])

    sent(RETURN)


def correlate(tile, peaks, valid):
    tables = host_tables()
    apart = pl.BlockSpec(memory_space=pltpu.HBM)
    count = 9 + STEPS + 1
    return pl.pallas_call(
        kernel,
        out_shape=jax.ShapeDtypeStruct((6, 10, 1, 10), F32),
        in_specs=[apart] * (3 + len(tables)),
        out_specs=pl.BlockSpec(memory_space=pltpu.VMEM),
        scratch_shapes=[
            pltpu.VMEM((ROWS, LANES), BF16),
            pltpu.VMEM((ROWS, LANES), BF16),
            pltpu.VMEM((MAIN // 2, 128), BF16),
            pltpu.VMEM((ROWS // 2, 128), BF16),
            pltpu.VMEM((ROWS // 2, 128), BF16),
            *[pltpu.VMEM(t.shape, t.dtype) for t in tables],
            pltpu.VMEM((ROWS, LANES), BF16),
            pltpu.VMEM((ROWS, LANES), BF16),
            pltpu.VMEM((ROWS, LANES), BF16),
            pltpu.VMEM((ROWS, LANES), BF16),
            pltpu.VMEM((10, 256, LANES), BF16),
            pltpu.VMEM((16, LANES), F32),
            pltpu.VMEM((16, LANES), F32),
            pltpu.VMEM((2, 10, 144, 128), F32),
            pltpu.VMEM((16, 8, 128), F32),
            pltpu.VMEM((10, 16, 128), F32),
            pltpu.VMEM((16, 128), F32),
            pltpu.VMEM((16, 128), F32),
            pltpu.VMEM((10, 2, 10), jnp.int32),
            pltpu.VMEM((10, 1, 10), jnp.int32),
            pltpu.SMEM((10, 2, 10), jnp.int32),
            pltpu.SemaphoreType.DMA((3 + len(tables),)),
            pltpu.SemaphoreType.DMA((count,)),
            pltpu.SemaphoreType.DMA((count,)),
        ],
        compiler_params=pltpu.CompilerParams(
            collective_id=0, has_side_effects=True, vmem_limit_bytes=62 * 1024 * 1024
        ),
    )(tile, peaks, valid, *[jnp.asarray(t) for t in tables])


def body(sections, peaks, valid):
    out = correlate(sections[0], jnp.transpose(peaks, (0, 2, 1, 3))[0], jnp.transpose(valid, (1, 0, 2)))
    return jnp.transpose(out, (2, 0, 1, 3))


def solution(mesh):
    in_specs = (P("gz", "gy", "gx"), P("gz", None, "gy", "gx"), P("gz", "gy", "gx"))
    out_specs = P("gz", None, "gy", "gx")
    return jax.shard_map(body, mesh=mesh, in_specs=in_specs, out_specs=out_specs, check_vma=False)
```

```python
import functools
import math

import jax
import jax.numpy as jnp
import ml_dtypes
import numpy as np
from jax import lax
from jax.experimental import pallas as pl
from jax.experimental.pallas import tpu as pltpu
from jax.sharding import PartitionSpec as P

PATCH = 128
STRIDE = 64
WIN = 5
HALF = 64
ROWS = 704
LANES = 768
BLOCKS = 5
STEPS = 5
F32 = jnp.float32
BF16 = jnp.bfloat16


def host_tables():
    index = np.arange(PATCH)
    phase = ((index[:, None] * index[None, :]) % PATCH).astype(np.float32) * np.float32(
        2.0 * math.pi / PATCH
    )
    rounded = lambda v: v.astype(ml_dtypes.bfloat16).astype(np.float32)
    cosine, sine = rounded(np.cos(phase)), rounded(np.sin(phase))
    first = np.zeros((256, 256), np.float32)
    last = np.zeros((256, 256), np.float32)
    weight = np.where(np.arange(HALF) == 0, 1.0, 2.0).astype(np.float32)
    for w in range(2):
        rows = slice(64 * w, 64 * w + 128)
        real, imag = slice(64 * w, 64 * w + 64), slice(128 + 64 * w, 192 + 64 * w)
        lags = slice(128 * w, 128 * w + 128)
        first[rows, real] = cosine[:HALF].T
        first[rows, imag] = -sine[:HALF].T
        first[rows, 128 + 64 * w] = 0.0
        last[real, lags] = (cosine[:, :HALF] * weight).T
        last[imag, lags] = (-sine[:, :HALF] * weight).T
        last[128 + 64 * w, lags] = cosine[:, HALF]
    nyquist = np.zeros((LANES, 128), np.float32)
    for b in range(BLOCKS):
        for w in range(2):
            start = 128 * b + 64 * w
            nyquist[start : start + 128, b + 64 * w] = cosine[HALF]
    forward = np.block([[cosine, sine], [-sine, cosine]])
    inverse = np.stack([np.block([[cosine, sine], [sine, -cosine]]), np.block([[cosine, -sine], [sine, cosine]])])
    offsets = np.arange(WIN, dtype=np.float32) - WIN // 2
    ones = np.ones(WIN, np.float32)
    square = offsets * offsets - np.mean(offsets * offsets)
    pairs = [(ones, ones), (offsets, ones), (ones, offsets), (square, ones), (ones, square), (offsets, offsets)]
    basis = np.zeros((6, 8, 128), np.float32)
    for e, (p, q) in enumerate(pairs):
        func = p[:, None] * q[None, :]
        func = func / np.sqrt(np.sum(func * func))
        for j in range(2 * BLOCKS):
            basis[e, :WIN, 8 * j : 8 * j + WIN] = func
    gather = np.zeros((128, 128), np.float32)
    for j in range(2 * BLOCKS):
        gather[8 * j : 8 * j + 8, j] = 1.0
    spread = np.zeros((LANES, 128), np.float32)
    for j in range(2 * BLOCKS):
        for e in range(6):
            spread[64 * j : 64 * j + 128, 16 * e + j] = 1.0
    low = lambda v: v.astype(ml_dtypes.bfloat16)
    return low(first), low(nyquist), low(forward), low(inverse), low(last), basis, gather, spread


def dot(a, b, precision=None):
    return lax.dot_general(a, b, (((1,), (0,)), ((), ())), precision=precision, preferred_element_type=F32)


def row_transform(x, first_ref, block):
    return dot(x[:, 128 * block : 128 * block + 256], first_ref[...]).astype(BF16)


def unpack(packed):
    wide = packed.astype(F32)
    return jnp.concatenate([wide, pltpu.roll(wide, HALF, 1)], 0).astype(BF16)


def square_sums(x, sums_ref, strip):
    x = x.astype(F32)
    sums_ref[pl.ds(strip, 1), :] = jnp.sum(x * x, axis=0, keepdims=True)


def column_transform(real_ref, imag_ref, start, forward_ref, lanes=slice(0, LANES)):
    data = jnp.concatenate([real_ref[pl.ds(start, 128), lanes], imag_ref[pl.ds(start, 128), lanes]], 0)
    return dot(forward_ref[...], data).astype(BF16)


MAIN = 640


class Place:
    def __init__(self):
        self.at = {name: lax.axis_index(name) for name in ("gz", "gx", "gy")}
        self.size = {name: lax.axis_size(name) for name in ("gz", "gx", "gy")}

    def there(self, step):
        inside = None
        for name, move in zip(("gz", "gx", "gy"), step):
            if not (isinstance(move, int) and move == 0):
                to = self.at[name] + move
                ok = jnp.logical_and(to >= 0, to < self.size[name])
                inside = ok if inside is None else jnp.logical_and(inside, ok)
        return inside

    def device(self, step):
        return {name: self.at[name] + move for name, move in zip(("gz", "gx", "gy"), step)}


def kernel(tile_ref, peaks_ref, valid_hbm, first_hbm, nyquist_hbm, forward_hbm, inverse_hbm, last_hbm, basis_hbm, gather_hbm,
           spread_hbm, out_ref,
           own, other, packed, own_edge, other_edge,
           first_ref, nyquist_ref, forward_ref, inverse_ref, last_ref, basis_ref, gather_ref, spread_ref,
           own_re, own_im, other_re, other_im, spectra, own_sums, other_sums, surface, windows, peak_rows,
           result, returned, far_peaks, valid, peaks, local_sems, send_sems, recv_sems):
    place = Place()
    second = 1 - lax.rem(place.at["gx"], 2)
    is_second = second == 1
    ahead = 2 * second - 1
    tables = [(first_hbm, first_ref), (nyquist_hbm, nyquist_ref), (forward_hbm, forward_ref), (inverse_hbm, inverse_ref),
              (last_hbm, last_ref), (basis_hbm, basis_ref), (gather_hbm, gather_ref), (spread_hbm, spread_ref)]
    main = pl.ds(0, MAIN)
    tile_copy = pltpu.make_async_copy(tile_ref, own.at[main, main], local_sems.at[0])
    local_peaks = pltpu.make_async_copy(peaks_ref, peaks, local_sems.at[1])
    tables.append((valid_hbm, valid))
    local = [pltpu.make_async_copy(a, b, local_sems.at[2 + n]) for n, (a, b) in enumerate(tables)]

    pair = place.there((-ahead, 0, 0))
    beside = place.there((0, 1, 0))
    top = pl.ds(0, STRIDE)
    low = pl.ds(MAIN, STRIDE)
    first32, last32 = pl.ds(0, 32), pl.ds(MAIN // 2, 32)
    copies = [
        ((0, 0, -1), (0, 0, 1), tile_ref.at[top, :], own.at[low, main], None),
        ((0, -1, 0), (0, 1, 0), packed, own_edge.at[pl.ds(0, MAIN // 2)], None),
        ((0, 0, -1), (0, 0, 1), own_edge.at[first32], own_edge.at[last32], beside),
        ((ahead, 0, 0), (-ahead, 0, 0), peaks_ref, far_peaks, is_second),
        ((-ahead, 0, 0), (ahead, 0, 0), result, returned, is_second),
        ((-ahead, -1, 0), (-ahead, 1, 0), packed.at[pl.ds(0, 96)], other_edge.at[pl.ds(0, 96)], None),
        ((-ahead, -1, 0), (-ahead, 1, 0), packed.at[pl.ds(96, 224)], other_edge.at[pl.ds(96, 224)], None),
        ((0, 0, -1), (0, 0, 1), other_edge.at[first32], other_edge.at[last32], jnp.logical_and(pair, beside)),
        ((0, 0, -1), (0, 0, 1), other.at[top, main], other.at[low, main], pair),
    ]
    FAR, RETURN, EDGE, LATER_EDGE, CORNER, FORWARD = 3, 4, 5, 6, 7, 8
    base = len(copies)
    for start, count in [(0, 64)] + [(64 + 128 * t, 128) for t in range(STEPS - 1)] + [(576, 64)]:
        rows = pl.ds(start, count)
        copies.append(((ahead, 0, 0), (-ahead, 0, 0), tile_ref.at[rows, :], other.at[rows, main], None))

    def remote(n):
        step, _, source, destination, _ = copies[n]
        return pltpu.make_async_remote_copy(
            src_ref=source, dst_ref=destination, send_sem=send_sems.at[n], recv_sem=recv_sems.at[n],
            device_id=place.device(step), device_id_type=pl.DeviceIdType.MESH,
        )

    def when(n, side):
        ok = place.there(copies[n][side])
        return ok if copies[n][4] is None else jnp.logical_and(ok, copies[n][4])

    def send(n):
        pl.when(when(n, 0))(lambda: remote(n).start())

    def sent(n):
        pl.when(when(n, 0))(lambda: remote(n).wait_send())

    def wait_for(n):
        pl.when(when(n, 1))(lambda: remote(n).wait_recv())

    @pl.when(place.at["gy"] == place.size["gy"] - 1)
    def _():
        own[MAIN:ROWS, :MAIN] = jnp.zeros((STRIDE, MAIN), BF16)
        own_edge[MAIN // 2 :, :] = jnp.zeros((32, 128), BF16)
        other[MAIN:ROWS, :MAIN] = jnp.zeros((STRIDE, MAIN), BF16)
        other_edge[MAIN // 2 :, :] = jnp.zeros((32, 128), BF16)

    @pl.when(place.at["gx"] == place.size["gx"] - 1)
    def _():
        own_edge[...] = jnp.zeros_like(own_edge)
        other_edge[...] = jnp.zeros_like(other_edge)

    @pl.when(jnp.logical_not(pair))
    def _():
        other[:, :MAIN] = jnp.zeros((ROWS, MAIN), BF16)
        other_edge[...] = jnp.zeros_like(other_edge)
        far_peaks[...] = jnp.zeros_like(far_peaks)

    @pl.when(place.at["gz"] == place.size["gz"] - 1)
    def _():
        returned[...] = jnp.zeros_like(returned)

    barrier = pltpu.get_barrier_semaphore()
    meetings = [((0, 0, -1), (0, 0, 1)), ((0, -1, 0), (0, 1, 0)), ((ahead, 0, 0), (-ahead, 0, 0)),
                ((-ahead, 0, 0), (ahead, 0, 0)), ((-ahead, -1, 0), (-ahead, 1, 0))]
    for _, step in meetings:
        @pl.when(place.there(step))
        def _():
            pl.semaphore_signal(barrier, inc=1, device_id=place.device(step), device_id_type=pl.DeviceIdType.MESH)
    tile_copy.start()
    for copy in local:
        copy.start()
    pl.when(jnp.logical_not(is_second))(lambda: local_peaks.start())
    left = lax.broadcasted_iota(jnp.int32, (32, 128), 1) < HALF
    tile_copy.wait()
    for n in range(MAIN // STRIDE):
        block = own[STRIDE * n : STRIDE * n + STRIDE, 0:128].astype(F32)
        packed[32 * n : 32 * n + 32, :] = jnp.where(left, block[:32], pltpu.roll(block[32:], HALF, 1)).astype(BF16)
    pl.semaphore_wait(barrier, sum(place.there(step).astype(jnp.int32) for step, _ in meetings))
    for n in (1, EDGE, 0, base, FAR, LATER_EDGE, *range(base + 1, len(copies))):
        send(n)

    windows[...] = jnp.zeros_like(windows)
    peak_rows[...] = jnp.zeros_like(peak_rows)
    for copy in local:
        copy.wait()

    def keep(re, im, rows, b, out):
        re[rows, 128 * b : 128 * b + 128] = out[:, :128]
        im[rows, 128 * b : 128 * b + 128] = out[:, 128:]

    def keep_nyquist(re, im, rows, out):
        re[rows, 128 * BLOCKS :] = out
        im[rows, 128 * BLOCKS :] = jnp.zeros((out.shape[0], 128), BF16)

    for b in range(BLOCKS - 1):
        keep(own_re, own_im, slice(0, MAIN), b, row_transform(own[0:MAIN, :], first_ref, b))
    near, distant = is_second, jnp.logical_not(is_second)

    def pass_own_corner():
        wait_for(1)
        send(2)

    def pass_corner():
        wait_for(EDGE)
        send(CORNER)

    pl.when(near)(pass_own_corner)
    wait_for(base)
    send(FORWARD)
    pl.when(near)(pass_corner)
    wait_for(0)
    for b in range(BLOCKS - 1):
        keep(own_re, own_im, slice(MAIN, ROWS), b, row_transform(own[MAIN:ROWS, :], first_ref, b))

    def own_spectra(lanes, count):
        def some(i, carry):
            for k in range(count):
                row = count * i + k
                start = pl.multiple_of(row * STRIDE, STRIDE)
                spectra[row, :, lanes] = column_transform(own_re, own_im, start, forward_ref, lanes)
            return carry

        lax.fori_loop(0, 10 // count, some, 0)

    pl.when(distant)(lambda: own_spectra(slice(0, 512), 5))
    pl.when(distant)(pass_own_corner)
    pl.when(distant)(pass_corner)
    wait_for(2)

    def own_strip(strip, carry):
        rows = pl.ds(pl.multiple_of(strip * STRIDE, STRIDE), STRIDE)
        own[rows, MAIN:] = unpack(own_edge[pl.ds(pl.multiple_of(strip * 32, 32), 32), :])
        square_sums(own[rows, :], own_sums, strip)
        return carry

    lax.fori_loop(0, ROWS // STRIDE, own_strip, 0)
    keep(own_re, own_im, slice(0, ROWS), BLOCKS - 1, row_transform(own[...], first_ref, BLOCKS - 1))
    keep_nyquist(own_re, own_im, slice(0, ROWS), dot(own[...], nyquist_ref[...]).astype(BF16))
    wait_for(FAR)
    far = pltpu.make_async_copy(far_peaks, peaks, local_sems.at[1])
    pl.when(is_second)(lambda: far.start())
    pl.when(near)(lambda: own_spectra(slice(0, LANES), 2))
    pl.when(distant)(lambda: own_spectra(slice(512, LANES), 10))
    pl.when(is_second)(lambda: far.wait())
    pl.when(jnp.logical_not(is_second))(lambda: local_peaks.wait())

    lane = lax.broadcasted_iota(jnp.int32, (128, 128), 1)
    slot = lax.rem(lane, HALF) == 0
    lane8 = lax.broadcasted_iota(jnp.int32, (8, 128), 1) // 8

    def other_rows(start, count):
        rows = pl.ds(pl.multiple_of(start, STRIDE), count)
        for k in range(count // STRIDE):
            strip = lax.div(start, STRIDE) + k
            here = pl.ds(pl.multiple_of(strip * STRIDE, STRIDE), STRIDE)
            edge = unpack(other_edge[pl.ds(pl.multiple_of(strip * 32, 32), 32), :])
            other[here, MAIN:] = edge
            square_sums(jnp.concatenate([other[here, :MAIN], edge], 1), other_sums, strip)
        x = other[rows, :]
        for b in range(BLOCKS):
            keep(other_re, other_im, rows, b, row_transform(x, first_ref, b))
        keep_nyquist(other_re, other_im, rows, dot(x, nyquist_ref[...]).astype(BF16))

    def patch_rows(rows):
        crosses = []
        for i in rows:
            a = spectra[i]
            b = column_transform(other_re, other_im, pl.multiple_of(i * STRIDE, STRIDE), forward_ref)
            ar, ai, br, bi = a[:128], a[128:], b[:128], b[128:]
            crosses.append(jnp.concatenate([ar * br + ai * bi, ar * bi - ai * br], 0))
        for k, i in enumerate(rows):
            turned = dot(inverse_ref[1 - second], crosses[k])
            extra = turned[:128, 128 * BLOCKS :]
            for b in range(BLOCKS):
                lanes = slice(128 * b, 128 * b + 128)
                moved = extra if b == 0 else pltpu.roll(extra, 128 - b, 1)
                imag = jnp.where(slot, moved, turned[128:, lanes]).astype(BF16)
                out = dot(jnp.concatenate([turned[:128, lanes].astype(BF16), imag], 1), last_ref[...])
                for w in range(2):
                    piece = out[:, 128 * w : 128 * w + 128]
                    j = 2 * b + w
                    surface[k, j, 8:136, :] = piece
                    surface[k, j, 0:8, :] = piece[120:]
                    surface[k, j, 136:144, :] = piece[:8]
                    peak_rows[j, pl.ds(i, 1), :] = jnp.max(jnp.abs(piece), axis=0, keepdims=True)
        for k, i in enumerate(rows):
            held = jnp.zeros((8, 128), F32)
            for j in range(2 * BLOCKS):
                dy = peaks[i, 0, j]
                dx = peaks[i, 1, j]
                piece = surface[k, j, pl.ds(dy + 6, 8), :]
                shift = lax.rem(8 * j + 2 + 128 - dx, 128)
                held = jnp.where(lane8 == j, pltpu.roll(piece, shift, 1), held)
            windows[i] = held

    high = lax.Precision.HIGHEST

    def energy(sums):
        return dot(sums[0:10, :] + sums[1:11, :], spread_ref[...], high) / float(PATCH * PATCH)

    own_energy = energy(own_sums)
    other_rows(jnp.int32(0), STRIDE)

    def step(t, carry):
        start = pl.multiple_of(128 * t + 64, 64)
        rows = other.at[pl.ds(start, 128), main]

        pl.when(t == 1)(lambda: wait_for(LATER_EDGE))

        @pl.when(pair)
        def _():
            pltpu.make_async_remote_copy(
                src_ref=rows, dst_ref=rows, send_sem=send_sems.at[base + 1 + t], recv_sem=recv_sems.at[base + 1 + t],
                device_id=place.device((0, 0, 0)), device_id_type=pl.DeviceIdType.MESH,
            ).wait_recv()

        other_rows(start, 128)
        patch_rows((2 * t, 2 * t + 1))
        return carry

    lax.fori_loop(0, STEPS - 1, step, 0)
    wait_for(base + STEPS)
    wait_for(FORWARD)
    wait_for(CORNER)
    other_rows(jnp.int32(576), 128)
    scale = float(PATCH) ** 3 * jnp.sqrt((own_energy + 1e-05) * (energy(other_sums) + 1e-05))
    patch_rows((8, 9))

    group = lax.rem(lax.broadcasted_iota(jnp.int32, (10, 128), 1), 16)
    peak = jnp.zeros((10, 128), F32)
    for j in range(2 * BLOCKS):
        peak = jnp.where(group == j, jnp.max(peak_rows[j, 0:10, :], axis=1, keepdims=True), peak)
    height = peak / scale + 1e-05
    sums = jnp.concatenate([jnp.sum(windows[...] * basis_ref[e][None], axis=1) for e in range(6)], 0)
    values = dot(sums, gather_ref[...], high)
    joined = values[0:16]
    for e in range(1, 6):
        joined = joined + pltpu.roll(values[16 * e : 16 * e + 16], 16 * e, 1)
    result[0:10, :] = joined[0:10] / scale / height
    send(RETURN)

    def give(coefficients):
        for e in range(6):
            moved = coefficients if e == 0 else pltpu.roll(coefficients, 128 - 16 * e, 1)
            out_ref[e, :, 0, :] = moved[0:10, :10] * valid[:, 0, :].astype(F32)

    for n in range(len(copies)):
        if n != RETURN:
            sent(n)

    @pl.when(jnp.logical_not(is_second))
    def _():
        give(result[...])

    @pl.when(is_second)
    def _():
        wait_for(RETURN)
        give(returned[...])

    sent(RETURN)


def correlate(tile, peaks, valid):
    tables = host_tables()
    apart = pl.BlockSpec(memory_space=pltpu.HBM)
    count = 9 + STEPS + 1
    return pl.pallas_call(
        kernel,
        out_shape=jax.ShapeDtypeStruct((6, 10, 1, 10), F32),
        in_specs=[apart] * (3 + len(tables)),
        out_specs=pl.BlockSpec(memory_space=pltpu.VMEM),
        scratch_shapes=[
            pltpu.VMEM((ROWS, LANES), BF16),
            pltpu.VMEM((ROWS, LANES), BF16),
            pltpu.VMEM((MAIN // 2, 128), BF16),
            pltpu.VMEM((ROWS // 2, 128), BF16),
            pltpu.VMEM((ROWS // 2, 128), BF16),
            *[pltpu.VMEM(t.shape, t.dtype) for t in tables],
            pltpu.VMEM((ROWS, LANES), BF16),
            pltpu.VMEM((ROWS, LANES), BF16),
            pltpu.VMEM((ROWS, LANES), BF16),
            pltpu.VMEM((ROWS, LANES), BF16),
            pltpu.VMEM((10, 256, LANES), BF16),
            pltpu.VMEM((16, LANES), F32),
            pltpu.VMEM((16, LANES), F32),
            pltpu.VMEM((2, 10, 144, 128), F32),
            pltpu.VMEM((16, 8, 128), F32),
            pltpu.VMEM((10, 16, 128), F32),
            pltpu.VMEM((16, 128), F32),
            pltpu.VMEM((16, 128), F32),
            pltpu.VMEM((10, 2, 10), jnp.int32),
            pltpu.VMEM((10, 1, 10), jnp.int32),
            pltpu.SMEM((10, 2, 10), jnp.int32),
            pltpu.SemaphoreType.DMA((3 + len(tables),)),
            pltpu.SemaphoreType.DMA((count,)),
            pltpu.SemaphoreType.DMA((count,)),
        ],
        compiler_params=pltpu.CompilerParams(
            collective_id=0, has_side_effects=True, vmem_limit_bytes=62 * 1024 * 1024
        ),
    )(tile, peaks, valid, *[jnp.asarray(t) for t in tables])


def body(sections, peaks, valid):
    out = correlate(sections[0], jnp.transpose(peaks, (0, 2, 1, 3))[0], jnp.transpose(valid, (1, 0, 2)))
    return jnp.transpose(out, (2, 0, 1, 3))


def solution(mesh):
    in_specs = (P("gz", "gy", "gx"), P("gz", None, "gy", "gx"), P("gz", "gy", "gx"))
    out_specs = P("gz", None, "gy", "gx")
    return jax.shard_map(body, mesh=mesh, in_specs=in_specs, out_specs=out_specs, check_vma=False)
```

```python
import functools
import math

import jax
import jax.numpy as jnp
import ml_dtypes
import numpy as np
from jax import lax
from jax.experimental import pallas as pl
from jax.experimental.pallas import tpu as pltpu
from jax.sharding import PartitionSpec as P

PATCH = 128
STRIDE = 64
WIN = 5
HALF = 64
ROWS = 704
LANES = 768
BLOCKS = 5
STEPS = 5
F32 = jnp.float32
BF16 = jnp.bfloat16


def host_tables():
    index = np.arange(PATCH)
    phase = ((index[:, None] * index[None, :]) % PATCH).astype(np.float32) * np.float32(
        2.0 * math.pi / PATCH
    )
    rounded = lambda v: v.astype(ml_dtypes.bfloat16).astype(np.float32)
    cosine, sine = rounded(np.cos(phase)), rounded(np.sin(phase))
    first = np.zeros((256, 256), np.float32)
    last = np.zeros((256, 256), np.float32)
    weight = np.where(np.arange(HALF) == 0, 1.0, 2.0).astype(np.float32)
    for w in range(2):
        rows = slice(64 * w, 64 * w + 128)
        real, imag = slice(64 * w, 64 * w + 64), slice(128 + 64 * w, 192 + 64 * w)
        lags = slice(128 * w, 128 * w + 128)
        first[rows, real] = cosine[:HALF].T
        first[rows, imag] = -sine[:HALF].T
        first[rows, 128 + 64 * w] = 0.0
        last[real, lags] = (cosine[:, :HALF] * weight).T
        last[imag, lags] = (-sine[:, :HALF] * weight).T
        last[128 + 64 * w, lags] = cosine[:, HALF]
    nyquist = np.zeros((LANES, 128), np.float32)
    for b in range(BLOCKS):
        for w in range(2):
            start = 128 * b + 64 * w
            nyquist[start : start + 128, b + 64 * w] = cosine[HALF]
    forward = np.block([[cosine, sine], [-sine, cosine]])
    inverse = np.stack([np.block([[cosine, sine], [sine, -cosine]]), np.block([[cosine, -sine], [sine, cosine]])])
    offsets = np.arange(WIN, dtype=np.float32) - WIN // 2
    ones = np.ones(WIN, np.float32)
    square = offsets * offsets - np.mean(offsets * offsets)
    pairs = [(ones, ones), (offsets, ones), (ones, offsets), (square, ones), (ones, square), (offsets, offsets)]
    basis = np.zeros((6, 8, 128), np.float32)
    for e, (p, q) in enumerate(pairs):
        func = p[:, None] * q[None, :]
        func = func / np.sqrt(np.sum(func * func))
        for j in range(2 * BLOCKS):
            basis[e, :WIN, 8 * j : 8 * j + WIN] = func
    gather = np.zeros((128, 128), np.float32)
    for j in range(2 * BLOCKS):
        gather[8 * j : 8 * j + 8, j] = 1.0
    spread = np.zeros((LANES, 128), np.float32)
    for j in range(2 * BLOCKS):
        for e in range(6):
            spread[64 * j : 64 * j + 128, 16 * e + j] = 1.0
    low = lambda v: v.astype(ml_dtypes.bfloat16)
    return low(first), low(nyquist), low(forward), low(inverse), low(last), basis, low(gather), low(spread)


def dot(a, b, precision=None):
    return lax.dot_general(a, b, (((1,), (0,)), ((), ())), precision=precision, preferred_element_type=F32)


def exact_dot(x, table):
    high = x.astype(BF16)
    rest = x - high.astype(F32)
    middle = rest.astype(BF16)
    low = (rest - middle.astype(F32)).astype(BF16)
    count = x.shape[0]
    out = dot(jnp.concatenate([high, middle, low], 0), table)
    return out[:count] + out[count : 2 * count] + out[2 * count :]


def row_transform(x, first_ref, block):
    return dot(x[:, 128 * block : 128 * block + 256], first_ref[...]).astype(BF16)


def unpack(packed):
    wide = packed.astype(F32)
    return jnp.concatenate([wide, pltpu.roll(wide, HALF, 1)], 0).astype(BF16)


def square_sums(x, sums_ref, strip):
    x = x.astype(F32)
    sums_ref[pl.ds(strip, 1), :] = jnp.sum(x * x, axis=0, keepdims=True)


def column_transform(real_ref, imag_ref, start, forward_ref, lanes=slice(0, LANES)):
    data = jnp.concatenate([real_ref[pl.ds(start, 128), lanes], imag_ref[pl.ds(start, 128), lanes]], 0)
    return dot(forward_ref[...], data).astype(BF16)


MAIN = 640


class Place:
    def __init__(self):
        self.at = {name: lax.axis_index(name) for name in ("gz", "gx", "gy")}
        self.size = {name: lax.axis_size(name) for name in ("gz", "gx", "gy")}

    def there(self, step):
        inside = None
        for name, move in zip(("gz", "gx", "gy"), step):
            if not (isinstance(move, int) and move == 0):
                to = self.at[name] + move
                ok = jnp.logical_and(to >= 0, to < self.size[name])
                inside = ok if inside is None else jnp.logical_and(inside, ok)
        return inside

    def device(self, step):
        return {name: self.at[name] + move for name, move in zip(("gz", "gx", "gy"), step)}


def kernel(tile_ref, peaks_ref, valid_hbm, first_hbm, nyquist_hbm, forward_hbm, inverse_hbm, last_hbm, basis_hbm, gather_hbm,
           spread_hbm, out_ref,
           own, other, packed, own_edge, other_edge,
           first_ref, nyquist_ref, forward_ref, inverse_ref, last_ref, basis_ref, gather_ref, spread_ref,
           own_re, own_im, other_re, other_im, spectra, own_sums, other_sums, surface, windows, peak_rows,
           result, returned, far_peaks, valid, peaks, local_sems, send_sems, recv_sems):
    place = Place()
    second = 1 - lax.rem(place.at["gx"], 2)
    is_second = second == 1
    ahead = 2 * second - 1
    tables = [(first_hbm, first_ref), (nyquist_hbm, nyquist_ref), (forward_hbm, forward_ref), (inverse_hbm, inverse_ref),
              (last_hbm, last_ref), (basis_hbm, basis_ref), (gather_hbm, gather_ref), (spread_hbm, spread_ref)]
    main = pl.ds(0, MAIN)
    tile_copy = pltpu.make_async_copy(tile_ref, own.at[main, main], local_sems.at[0])
    local_peaks = pltpu.make_async_copy(peaks_ref, peaks, local_sems.at[1])
    tables.append((valid_hbm, valid))
    local = [pltpu.make_async_copy(a, b, local_sems.at[2 + n]) for n, (a, b) in enumerate(tables)]

    pair = place.there((-ahead, 0, 0))
    beside = place.there((0, 1, 0))
    top = pl.ds(0, STRIDE)
    low = pl.ds(MAIN, STRIDE)
    first32, last32 = pl.ds(0, 32), pl.ds(MAIN // 2, 32)
    copies = [
        ((0, 0, -1), (0, 0, 1), tile_ref.at[top, :], own.at[low, main], None),
        ((0, -1, 0), (0, 1, 0), packed, own_edge.at[pl.ds(0, MAIN // 2)], None),
        ((0, 0, -1), (0, 0, 1), own_edge.at[first32], own_edge.at[last32], beside),
        ((ahead, 0, 0), (-ahead, 0, 0), peaks_ref, far_peaks, is_second),
        ((-ahead, 0, 0), (ahead, 0, 0), result, returned, is_second),
        ((-ahead, -1, 0), (-ahead, 1, 0), packed.at[pl.ds(0, 96)], other_edge.at[pl.ds(0, 96)], None),
        ((-ahead, -1, 0), (-ahead, 1, 0), packed.at[pl.ds(96, 224)], other_edge.at[pl.ds(96, 224)], None),
        ((0, 0, -1), (0, 0, 1), other_edge.at[first32], other_edge.at[last32], jnp.logical_and(pair, beside)),
        ((0, 0, -1), (0, 0, 1), other.at[top, main], other.at[low, main], pair),
    ]
    FAR, RETURN, EDGE, LATER_EDGE, CORNER, FORWARD = 3, 4, 5, 6, 7, 8
    base = len(copies)
    for start, count in [(0, 64)] + [(64 + 128 * t, 128) for t in range(STEPS - 1)] + [(576, 64)]:
        rows = pl.ds(start, count)
        copies.append(((ahead, 0, 0), (-ahead, 0, 0), tile_ref.at[rows, :], other.at[rows, main], None))

    def remote(n):
        step, _, source, destination, _ = copies[n]
        return pltpu.make_async_remote_copy(
            src_ref=source, dst_ref=destination, send_sem=send_sems.at[n], recv_sem=recv_sems.at[n],
            device_id=place.device(step), device_id_type=pl.DeviceIdType.MESH,
        )

    def when(n, side):
        ok = place.there(copies[n][side])
        return ok if copies[n][4] is None else jnp.logical_and(ok, copies[n][4])

    def send(n):
        pl.when(when(n, 0))(lambda: remote(n).start())

    def sent(n):
        pl.when(when(n, 0))(lambda: remote(n).wait_send())

    def wait_for(n):
        pl.when(when(n, 1))(lambda: remote(n).wait_recv())

    @pl.when(place.at["gy"] == place.size["gy"] - 1)
    def _():
        own[MAIN:ROWS, :MAIN] = jnp.zeros((STRIDE, MAIN), BF16)
        own_edge[MAIN // 2 :, :] = jnp.zeros((32, 128), BF16)
        other[MAIN:ROWS, :MAIN] = jnp.zeros((STRIDE, MAIN), BF16)
        other_edge[MAIN // 2 :, :] = jnp.zeros((32, 128), BF16)

    @pl.when(place.at["gx"] == place.size["gx"] - 1)
    def _():
        own_edge[...] = jnp.zeros_like(own_edge)
        other_edge[...] = jnp.zeros_like(other_edge)

    @pl.when(jnp.logical_not(pair))
    def _():
        other[:, :MAIN] = jnp.zeros((ROWS, MAIN), BF16)
        other_edge[...] = jnp.zeros_like(other_edge)
        far_peaks[...] = jnp.zeros_like(far_peaks)

    @pl.when(place.at["gz"] == place.size["gz"] - 1)
    def _():
        returned[...] = jnp.zeros_like(returned)

    barrier = pltpu.get_barrier_semaphore()
    meetings = [((0, 0, -1), (0, 0, 1)), ((0, -1, 0), (0, 1, 0)), ((ahead, 0, 0), (-ahead, 0, 0)),
                ((-ahead, 0, 0), (ahead, 0, 0)), ((-ahead, -1, 0), (-ahead, 1, 0))]
    for _, step in meetings:
        @pl.when(place.there(step))
        def _():
            pl.semaphore_signal(barrier, inc=1, device_id=place.device(step), device_id_type=pl.DeviceIdType.MESH)
    tile_copy.start()
    for copy in local:
        copy.start()
    pl.when(jnp.logical_not(is_second))(lambda: local_peaks.start())
    left = lax.broadcasted_iota(jnp.int32, (32, 128), 1) < HALF
    tile_copy.wait()
    for n in range(MAIN // STRIDE):
        block = own[STRIDE * n : STRIDE * n + STRIDE, 0:128].astype(F32)
        packed[32 * n : 32 * n + 32, :] = jnp.where(left, block[:32], pltpu.roll(block[32:], HALF, 1)).astype(BF16)
    pl.semaphore_wait(barrier, sum(place.there(step).astype(jnp.int32) for step, _ in meetings))
    for n in (1, EDGE, 0, base, FAR, LATER_EDGE, *range(base + 1, len(copies))):
        send(n)

    windows[...] = jnp.zeros_like(windows)
    peak_rows[...] = jnp.zeros_like(peak_rows)
    for copy in local:
        copy.wait()

    def keep(re, im, rows, b, out):
        re[rows, 128 * b : 128 * b + 128] = out[:, :128]
        im[rows, 128 * b : 128 * b + 128] = out[:, 128:]

    def keep_nyquist(re, im, rows, out):
        re[rows, 128 * BLOCKS :] = out
        im[rows, 128 * BLOCKS :] = jnp.zeros((out.shape[0], 128), BF16)

    for b in range(BLOCKS - 1):
        keep(own_re, own_im, slice(0, MAIN), b, row_transform(own[0:MAIN, :], first_ref, b))
    near, distant = is_second, jnp.logical_not(is_second)

    def pass_own_corner():
        wait_for(1)
        send(2)

    def pass_corner():
        wait_for(EDGE)
        send(CORNER)

    pl.when(near)(pass_own_corner)
    wait_for(base)
    send(FORWARD)
    pl.when(near)(pass_corner)
    wait_for(0)
    for b in range(BLOCKS - 1):
        keep(own_re, own_im, slice(MAIN, ROWS), b, row_transform(own[MAIN:ROWS, :], first_ref, b))

    def own_spectra(lanes, count):
        def some(i, carry):
            for k in range(count):
                row = count * i + k
                start = pl.multiple_of(row * STRIDE, STRIDE)
                spectra[row, :, lanes] = column_transform(own_re, own_im, start, forward_ref, lanes)
            return carry

        lax.fori_loop(0, 10 // count, some, 0)

    pl.when(distant)(lambda: own_spectra(slice(0, 512), 10))
    pl.when(distant)(pass_own_corner)
    pl.when(distant)(pass_corner)
    wait_for(2)

    def own_strip(strip, carry):
        rows = pl.ds(pl.multiple_of(strip * STRIDE, STRIDE), STRIDE)
        own[rows, MAIN:] = unpack(own_edge[pl.ds(pl.multiple_of(strip * 32, 32), 32), :])
        square_sums(own[rows, :], own_sums, strip)
        return carry

    lax.fori_loop(0, ROWS // STRIDE, own_strip, 0, unroll=True)
    keep(own_re, own_im, slice(0, ROWS), BLOCKS - 1, row_transform(own[...], first_ref, BLOCKS - 1))
    keep_nyquist(own_re, own_im, slice(0, ROWS), dot(own[...], nyquist_ref[...]).astype(BF16))
    wait_for(FAR)
    far = pltpu.make_async_copy(far_peaks, peaks, local_sems.at[1])
    pl.when(is_second)(lambda: far.start())
    pl.when(near)(lambda: own_spectra(slice(0, LANES), 10))
    pl.when(distant)(lambda: own_spectra(slice(512, LANES), 10))
    pl.when(is_second)(lambda: far.wait())
    pl.when(jnp.logical_not(is_second))(lambda: local_peaks.wait())

    lane = lax.broadcasted_iota(jnp.int32, (128, 128), 1)
    slot = lax.rem(lane, HALF) == 0
    lane8 = lax.broadcasted_iota(jnp.int32, (8, 128), 1) // 8

    def other_rows(start, count):
        rows = pl.ds(pl.multiple_of(start, STRIDE), count)
        for k in range(count // STRIDE):
            strip = lax.div(start, STRIDE) + k
            here = pl.ds(pl.multiple_of(strip * STRIDE, STRIDE), STRIDE)
            edge = unpack(other_edge[pl.ds(pl.multiple_of(strip * 32, 32), 32), :])
            other[here, MAIN:] = edge
            square_sums(jnp.concatenate([other[here, :MAIN], edge], 1), other_sums, strip)
        x = other[rows, :]
        for b in range(BLOCKS):
            keep(other_re, other_im, rows, b, row_transform(x, first_ref, b))
        keep_nyquist(other_re, other_im, rows, dot(x, nyquist_ref[...]).astype(BF16))

    def patch_rows(rows):
        crosses = []
        for i in rows:
            a = spectra[i]
            b = column_transform(other_re, other_im, pl.multiple_of(i * STRIDE, STRIDE), forward_ref)
            ar, ai, br, bi = a[:128], a[128:], b[:128], b[128:]
            crosses.append(jnp.concatenate([ar * br + ai * bi, ar * bi - ai * br], 0))
        for k, i in enumerate(rows):
            turned = dot(inverse_ref[1 - second], crosses[k])
            extra = turned[:128, 128 * BLOCKS :]
            for b in range(BLOCKS):
                lanes = slice(128 * b, 128 * b + 128)
                moved = extra if b == 0 else pltpu.roll(extra, 128 - b, 1)
                imag = jnp.where(slot, moved, turned[128:, lanes]).astype(BF16)
                out = dot(jnp.concatenate([turned[:128, lanes].astype(BF16), imag], 1), last_ref[...])
                for w in range(2):
                    piece = out[:, 128 * w : 128 * w + 128]
                    j = 2 * b + w
                    surface[k, j, 8:136, :] = piece
                    surface[k, j, 0:8, :] = piece[120:]
                    surface[k, j, 136:144, :] = piece[:8]
                    peak_rows[j, pl.ds(i, 1), :] = jnp.max(jnp.abs(piece), axis=0, keepdims=True)
        for k, i in enumerate(rows):
            held = jnp.zeros((8, 128), F32)
            for j in range(2 * BLOCKS):
                dy = peaks[i, 0, j]
                dx = peaks[i, 1, j]
                piece = surface[k, j, pl.ds(dy + 6, 8), :]
                shift = lax.rem(8 * j + 2 + 128 - dx, 128)
                held = jnp.where(lane8 == j, pltpu.roll(piece, shift, 1), held)
            windows[i] = held

    def energy(sums):
        rows = jnp.concatenate([sums[0:10, :] + sums[1:11, :], jnp.zeros((6, LANES), F32)], 0)
        return exact_dot(rows, spread_ref[...])[0:10] / float(PATCH * PATCH)

    own_energy = energy(own_sums)
    other_rows(jnp.int32(0), STRIDE)

    def step(t, carry):
        start = pl.multiple_of(128 * t + 64, 64)
        rows = other.at[pl.ds(start, 128), main]

        pl.when(t == 1)(lambda: wait_for(LATER_EDGE))

        @pl.when(pair)
        def _():
            pltpu.make_async_remote_copy(
                src_ref=rows, dst_ref=rows, send_sem=send_sems.at[base + 1 + t], recv_sem=recv_sems.at[base + 1 + t],
                device_id=place.device((0, 0, 0)), device_id_type=pl.DeviceIdType.MESH,
            ).wait_recv()

        other_rows(start, 128)
        patch_rows((2 * t, 2 * t + 1))
        return carry

    lax.fori_loop(0, STEPS - 1, step, 0)
    wait_for(base + STEPS)
    wait_for(FORWARD)
    wait_for(CORNER)
    other_rows(jnp.int32(576), 128)
    scale = float(PATCH) ** 3 * jnp.sqrt((own_energy + 1e-05) * (energy(other_sums) + 1e-05))
    patch_rows((8, 9))

    group = lax.rem(lax.broadcasted_iota(jnp.int32, (10, 128), 1), 16)
    peak = jnp.zeros((10, 128), F32)
    for j in range(2 * BLOCKS):
        peak = jnp.where(group == j, jnp.max(peak_rows[j, 0:10, :], axis=1, keepdims=True), peak)
    height = peak / scale + 1e-05
    sums = jnp.concatenate([jnp.sum(windows[...] * basis_ref[e][None], axis=1) for e in range(6)], 0)
    values = exact_dot(sums, gather_ref[...])
    joined = values[0:16]
    for e in range(1, 6):
        joined = joined + pltpu.roll(values[16 * e : 16 * e + 16], 16 * e, 1)
    result[0:10, :] = joined[0:10] / scale / height
    send(RETURN)

    def give(coefficients):
        for e in range(6):
            moved = coefficients if e == 0 else pltpu.roll(coefficients, 128 - 16 * e, 1)
            out_ref[e, :, 0, :] = moved[0:10, :10] * valid[:, 0, :].astype(F32)

    for n in range(len(copies)):
        if n != RETURN:
            sent(n)

    @pl.when(jnp.logical_not(is_second))
    def _():
        give(result[...])

    @pl.when(is_second)
    def _():
        wait_for(RETURN)
        give(returned[...])

    sent(RETURN)


def correlate(tile, peaks, valid):
    tables = host_tables()
    apart = pl.BlockSpec(memory_space=pltpu.HBM)
    count = 9 + STEPS + 1
    return pl.pallas_call(
        kernel,
        out_shape=jax.ShapeDtypeStruct((6, 10, 1, 10), F32),
        in_specs=[apart] * (3 + len(tables)),
        out_specs=pl.BlockSpec(memory_space=pltpu.VMEM),
        scratch_shapes=[
            pltpu.VMEM((ROWS, LANES), BF16),
            pltpu.VMEM((ROWS, LANES), BF16),
            pltpu.VMEM((MAIN // 2, 128), BF16),
            pltpu.VMEM((ROWS // 2, 128), BF16),
            pltpu.VMEM((ROWS // 2, 128), BF16),
            *[pltpu.VMEM(t.shape, t.dtype) for t in tables],
            pltpu.VMEM((ROWS, LANES), BF16),
            pltpu.VMEM((ROWS, LANES), BF16),
            pltpu.VMEM((ROWS, LANES), BF16),
            pltpu.VMEM((ROWS, LANES), BF16),
            pltpu.VMEM((10, 256, LANES), BF16),
            pltpu.VMEM((16, LANES), F32),
            pltpu.VMEM((16, LANES), F32),
            pltpu.VMEM((2, 10, 144, 128), F32),
            pltpu.VMEM((16, 8, 128), F32),
            pltpu.VMEM((10, 16, 128), F32),
            pltpu.VMEM((16, 128), F32),
            pltpu.VMEM((16, 128), F32),
            pltpu.VMEM((10, 2, 10), jnp.int32),
            pltpu.VMEM((10, 1, 10), jnp.int32),
            pltpu.SMEM((10, 2, 10), jnp.int32),
            pltpu.SemaphoreType.DMA((3 + len(tables),)),
            pltpu.SemaphoreType.DMA((count,)),
            pltpu.SemaphoreType.DMA((count,)),
        ],
        compiler_params=pltpu.CompilerParams(
            collective_id=0, has_side_effects=True, vmem_limit_bytes=62 * 1024 * 1024
        ),
    )(tile, peaks, valid, *[jnp.asarray(t) for t in tables])


def body(sections, peaks, valid):
    out = correlate(sections[0], jnp.transpose(peaks, (0, 2, 1, 3))[0], jnp.transpose(valid, (1, 0, 2)))
    return jnp.transpose(out, (2, 0, 1, 3))


def solution(mesh):
    in_specs = (P("gz", "gy", "gx"), P("gz", None, "gy", "gx"), P("gz", "gy", "gx"))
    out_specs = P("gz", None, "gy", "gx")
    return jax.shard_map(body, mesh=mesh, in_specs=in_specs, out_specs=out_specs, check_vma=False)
```

```python
import functools
import math

import jax
import jax.numpy as jnp
import ml_dtypes
import numpy as np
from jax import lax
from jax.experimental import pallas as pl
from jax.experimental.pallas import tpu as pltpu
from jax.sharding import PartitionSpec as P

PATCH = 128
STRIDE = 64
WIN = 5
HALF = 64
ROWS = 704
LANES = 768
BLOCKS = 5
STEPS = 5
F32 = jnp.float32
BF16 = jnp.bfloat16


def host_tables():
    index = np.arange(PATCH)
    phase = ((index[:, None] * index[None, :]) % PATCH).astype(np.float32) * np.float32(
        2.0 * math.pi / PATCH
    )
    rounded = lambda v: v.astype(ml_dtypes.bfloat16).astype(np.float32)
    cosine, sine = rounded(np.cos(phase)), rounded(np.sin(phase))
    first = np.zeros((256, 256), np.float32)
    last = np.zeros((256, 256), np.float32)
    weight = np.where(np.arange(HALF) == 0, 1.0, 2.0).astype(np.float32)
    for w in range(2):
        rows = slice(64 * w, 64 * w + 128)
        real, imag = slice(64 * w, 64 * w + 64), slice(128 + 64 * w, 192 + 64 * w)
        lags = slice(128 * w, 128 * w + 128)
        first[rows, real] = cosine[:HALF].T
        first[rows, imag] = -sine[:HALF].T
        first[rows, 128 + 64 * w] = 0.0
        last[real, lags] = (cosine[:, :HALF] * weight).T
        last[imag, lags] = (-sine[:, :HALF] * weight).T
        last[128 + 64 * w, lags] = cosine[:, HALF]
    nyquist = np.zeros((LANES, 128), np.float32)
    for b in range(BLOCKS):
        for w in range(2):
            start = 128 * b + 64 * w
            nyquist[start : start + 128, b + 64 * w] = cosine[HALF]
    forward = np.block([[cosine, sine], [-sine, cosine]])
    inverse = np.stack([np.block([[cosine, sine], [sine, -cosine]]), np.block([[cosine, -sine], [sine, cosine]])])
    offsets = np.arange(WIN, dtype=np.float32) - WIN // 2
    ones = np.ones(WIN, np.float32)
    square = offsets * offsets - np.mean(offsets * offsets)
    pairs = [(ones, ones), (offsets, ones), (ones, offsets), (square, ones), (ones, square), (offsets, offsets)]
    basis = np.zeros((6, 8, 128), np.float32)
    for e, (p, q) in enumerate(pairs):
        func = p[:, None] * q[None, :]
        func = func / np.sqrt(np.sum(func * func))
        for j in range(2 * BLOCKS):
            basis[e, :WIN, 8 * j : 8 * j + WIN] = func
    gather = np.zeros((128, 128), np.float32)
    for j in range(2 * BLOCKS):
        gather[8 * j : 8 * j + 8, j] = 1.0
    spread = np.zeros((LANES, 128), np.float32)
    for j in range(2 * BLOCKS):
        for e in range(6):
            spread[64 * j : 64 * j + 128, 16 * e + j] = 1.0
    low = lambda v: v.astype(ml_dtypes.bfloat16)
    return low(first), low(nyquist), low(forward), low(inverse), low(last), basis, low(gather), low(spread)


def dot(a, b, precision=None):
    return lax.dot_general(a, b, (((1,), (0,)), ((), ())), precision=precision, preferred_element_type=F32)


def exact_dot(x, table):
    high = x.astype(BF16)
    rest = x - high.astype(F32)
    middle = rest.astype(BF16)
    low = (rest - middle.astype(F32)).astype(BF16)
    count = x.shape[0]
    out = dot(jnp.concatenate([high, middle, low], 0), table)
    return out[:count] + out[count : 2 * count] + out[2 * count :]


def row_transform(x, first_ref, block):
    return dot(x[:, 128 * block : 128 * block + 256], first_ref[...]).astype(BF16)


def unpack(packed):
    wide = packed.astype(F32)
    return jnp.concatenate([wide, pltpu.roll(wide, HALF, 1)], 0).astype(BF16)


def square_sums(x, sums_ref, strip):
    x = x.astype(F32)
    sums_ref[pl.ds(strip, 1), :] = jnp.sum(x * x, axis=0, keepdims=True)


def column_transform(real_ref, imag_ref, start, forward_ref, lanes=slice(0, LANES)):
    data = jnp.concatenate([real_ref[pl.ds(start, 128), lanes], imag_ref[pl.ds(start, 128), lanes]], 0)
    return dot(forward_ref[...], data).astype(BF16)


MAIN = 640


class Place:
    def __init__(self):
        self.at = {name: lax.axis_index(name) for name in ("gz", "gx", "gy")}
        self.size = {name: lax.axis_size(name) for name in ("gz", "gx", "gy")}

    def there(self, step):
        inside = None
        for name, move in zip(("gz", "gx", "gy"), step):
            if not (isinstance(move, int) and move == 0):
                to = self.at[name] + move
                ok = jnp.logical_and(to >= 0, to < self.size[name])
                inside = ok if inside is None else jnp.logical_and(inside, ok)
        return inside

    def device(self, step):
        return {name: self.at[name] + move for name, move in zip(("gz", "gx", "gy"), step)}


def kernel(tile_ref, peaks_ref, valid_hbm, first_hbm, nyquist_hbm, forward_hbm, inverse_hbm, last_hbm, basis_hbm, gather_hbm,
           spread_hbm, out_ref,
           own, other, packed, own_edge, other_edge,
           first_ref, nyquist_ref, forward_ref, inverse_ref, last_ref, basis_ref, gather_ref, spread_ref,
           own_re, own_im, other_re, other_im, spectra, own_sums, other_sums, surface, windows, peak_rows,
           result, returned, far_peaks, valid, peaks, local_sems, send_sems, recv_sems):
    place = Place()
    second = 1 - lax.rem(place.at["gx"], 2)
    is_second = second == 1
    ahead = 2 * second - 1
    tables = [(first_hbm, first_ref), (nyquist_hbm, nyquist_ref), (forward_hbm, forward_ref), (inverse_hbm, inverse_ref),
              (last_hbm, last_ref), (basis_hbm, basis_ref), (gather_hbm, gather_ref), (spread_hbm, spread_ref)]
    main = pl.ds(0, MAIN)
    tile_copy = pltpu.make_async_copy(tile_ref, own.at[main, main], local_sems.at[0])
    local_peaks = pltpu.make_async_copy(peaks_ref, peaks, local_sems.at[1])
    tables.append((valid_hbm, valid))
    local = [pltpu.make_async_copy(a, b, local_sems.at[2 + n]) for n, (a, b) in enumerate(tables)]

    pair = place.there((-ahead, 0, 0))
    beside = place.there((0, 1, 0))
    top = pl.ds(0, STRIDE)
    low = pl.ds(MAIN, STRIDE)
    first32, last32 = pl.ds(0, 32), pl.ds(MAIN // 2, 32)
    copies = [
        ((0, 0, -1), (0, 0, 1), tile_ref.at[top, :], own.at[low, main], None),
        ((0, -1, 0), (0, 1, 0), packed, own_edge.at[pl.ds(0, MAIN // 2)], None),
        ((0, 0, -1), (0, 0, 1), own_edge.at[first32], own_edge.at[last32], beside),
        ((ahead, 0, 0), (-ahead, 0, 0), peaks_ref, far_peaks, is_second),
        ((-ahead, 0, 0), (ahead, 0, 0), result, returned, is_second),
        ((-ahead, -1, 0), (-ahead, 1, 0), packed.at[pl.ds(0, 96)], other_edge.at[pl.ds(0, 96)], None),
        ((-ahead, -1, 0), (-ahead, 1, 0), packed.at[pl.ds(96, 224)], other_edge.at[pl.ds(96, 224)], None),
        ((0, 0, -1), (0, 0, 1), other_edge.at[first32], other_edge.at[last32], jnp.logical_and(pair, beside)),
        ((0, 0, -1), (0, 0, 1), other.at[top, main], other.at[low, main], pair),
    ]
    FAR, RETURN, EDGE, LATER_EDGE, CORNER, FORWARD = 3, 4, 5, 6, 7, 8
    base = len(copies)
    for start, count in [(0, 64)] + [(64 + 128 * t, 128) for t in range(STEPS - 1)] + [(576, 64)]:
        rows = pl.ds(start, count)
        copies.append(((ahead, 0, 0), (-ahead, 0, 0), tile_ref.at[rows, :], other.at[rows, main], None))

    def remote(n):
        step, _, source, destination, _ = copies[n]
        return pltpu.make_async_remote_copy(
            src_ref=source, dst_ref=destination, send_sem=send_sems.at[n], recv_sem=recv_sems.at[n],
            device_id=place.device(step), device_id_type=pl.DeviceIdType.MESH,
        )

    def when(n, side):
        ok = place.there(copies[n][side])
        return ok if copies[n][4] is None else jnp.logical_and(ok, copies[n][4])

    def send(n):
        pl.when(when(n, 0))(lambda: remote(n).start())

    def sent(n):
        pl.when(when(n, 0))(lambda: remote(n).wait_send())

    def wait_for(n):
        pl.when(when(n, 1))(lambda: remote(n).wait_recv())

    @pl.when(place.at["gy"] == place.size["gy"] - 1)
    def _():
        own[MAIN:ROWS, :MAIN] = jnp.zeros((STRIDE, MAIN), BF16)
        own_edge[MAIN // 2 :, :] = jnp.zeros((32, 128), BF16)
        other[MAIN:ROWS, :MAIN] = jnp.zeros((STRIDE, MAIN), BF16)
        other_edge[MAIN // 2 :, :] = jnp.zeros((32, 128), BF16)

    @pl.when(place.at["gx"] == place.size["gx"] - 1)
    def _():
        own_edge[...] = jnp.zeros_like(own_edge)
        other_edge[...] = jnp.zeros_like(other_edge)

    @pl.when(jnp.logical_not(pair))
    def _():
        other[:, :MAIN] = jnp.zeros((ROWS, MAIN), BF16)
        other_edge[...] = jnp.zeros_like(other_edge)
        far_peaks[...] = jnp.zeros_like(far_peaks)

    @pl.when(place.at["gz"] == place.size["gz"] - 1)
    def _():
        returned[...] = jnp.zeros_like(returned)

    barrier = pltpu.get_barrier_semaphore()
    meetings = [((0, 0, -1), (0, 0, 1)), ((0, -1, 0), (0, 1, 0)), ((ahead, 0, 0), (-ahead, 0, 0)),
                ((-ahead, 0, 0), (ahead, 0, 0)), ((-ahead, -1, 0), (-ahead, 1, 0))]
    for _, step in meetings:
        @pl.when(place.there(step))
        def _():
            pl.semaphore_signal(barrier, inc=1, device_id=place.device(step), device_id_type=pl.DeviceIdType.MESH)
    tile_copy.start()
    for copy in local:
        copy.start()
    pl.when(jnp.logical_not(is_second))(lambda: local_peaks.start())
    left = lax.broadcasted_iota(jnp.int32, (32, 128), 1) < HALF
    tile_copy.wait()
    for n in range(MAIN // STRIDE):
        block = own[STRIDE * n : STRIDE * n + STRIDE, 0:128].astype(F32)
        packed[32 * n : 32 * n + 32, :] = jnp.where(left, block[:32], pltpu.roll(block[32:], HALF, 1)).astype(BF16)
    pl.semaphore_wait(barrier, sum(place.there(step).astype(jnp.int32) for step, _ in meetings))
    for n in (1, EDGE, 0, base, FAR, LATER_EDGE, *range(base + 1, len(copies))):
        send(n)

    windows[...] = jnp.zeros_like(windows)
    peak_rows[...] = jnp.zeros_like(peak_rows)
    for copy in local:
        copy.wait()

    def keep(re, im, rows, b, out):
        re[rows, 128 * b : 128 * b + 128] = out[:, :128]
        im[rows, 128 * b : 128 * b + 128] = out[:, 128:]

    def keep_nyquist(re, im, rows, out):
        re[rows, 128 * BLOCKS :] = out
        im[rows, 128 * BLOCKS :] = jnp.zeros((out.shape[0], 128), BF16)

    for b in range(BLOCKS - 1):
        keep(own_re, own_im, slice(0, MAIN), b, row_transform(own[0:MAIN, :], first_ref, b))
    near, distant = is_second, jnp.logical_not(is_second)

    def pass_own_corner():
        wait_for(1)
        send(2)

    def pass_corner():
        wait_for(EDGE)
        send(CORNER)

    pl.when(near)(pass_own_corner)
    wait_for(base)
    send(FORWARD)
    pl.when(near)(pass_corner)
    wait_for(0)
    for b in range(BLOCKS - 1):
        keep(own_re, own_im, slice(MAIN, ROWS), b, row_transform(own[MAIN:ROWS, :], first_ref, b))

    def own_spectra(lanes, count):
        def some(i, carry):
            for k in range(count):
                row = count * i + k
                start = pl.multiple_of(row * STRIDE, STRIDE)
                spectra[row, :, lanes] = column_transform(own_re, own_im, start, forward_ref, lanes)
            return carry

        lax.fori_loop(0, 10 // count, some, 0)

    pl.when(distant)(lambda: own_spectra(slice(0, 512), 10))
    pl.when(distant)(pass_own_corner)
    pl.when(distant)(pass_corner)
    wait_for(2)

    def own_strip(strip, carry):
        rows = pl.ds(pl.multiple_of(strip * STRIDE, STRIDE), STRIDE)
        own[rows, MAIN:] = unpack(own_edge[pl.ds(pl.multiple_of(strip * 32, 32), 32), :])
        square_sums(own[rows, :], own_sums, strip)
        return carry

    lax.fori_loop(0, ROWS // STRIDE, own_strip, 0, unroll=True)
    keep(own_re, own_im, slice(0, ROWS), BLOCKS - 1, row_transform(own[...], first_ref, BLOCKS - 1))
    keep_nyquist(own_re, own_im, slice(0, ROWS), dot(own[...], nyquist_ref[...]).astype(BF16))
    wait_for(FAR)
    far = pltpu.make_async_copy(far_peaks, peaks, local_sems.at[1])
    pl.when(is_second)(lambda: far.start())
    pl.when(near)(lambda: own_spectra(slice(0, LANES), 10))
    pl.when(distant)(lambda: own_spectra(slice(512, LANES), 10))
    pl.when(is_second)(lambda: far.wait())
    pl.when(jnp.logical_not(is_second))(lambda: local_peaks.wait())

    lane = lax.broadcasted_iota(jnp.int32, (128, 128), 1)
    slot = lax.rem(lane, HALF) == 0
    lane8 = lax.broadcasted_iota(jnp.int32, (8, 128), 1) // 8

    def other_rows(start, count):
        rows = pl.ds(pl.multiple_of(start, STRIDE), count)
        for k in range(count // STRIDE):
            strip = lax.div(start, STRIDE) + k
            here = pl.ds(pl.multiple_of(strip * STRIDE, STRIDE), STRIDE)
            edge = unpack(other_edge[pl.ds(pl.multiple_of(strip * 32, 32), 32), :])
            other[here, MAIN:] = edge
            square_sums(jnp.concatenate([other[here, :MAIN], edge], 1), other_sums, strip)
        x = other[rows, :]
        for b in range(BLOCKS):
            keep(other_re, other_im, rows, b, row_transform(x, first_ref, b))
        keep_nyquist(other_re, other_im, rows, dot(x, nyquist_ref[...]).astype(BF16))

    def patch_rows(rows):
        crosses = []
        theirs = [column_transform(other_re, other_im, pl.multiple_of(i * STRIDE, STRIDE), forward_ref) for i in rows]
        for i, b in zip(rows, theirs):
            a = spectra[i]
            ar, ai, br, bi = a[:128], a[128:], b[:128], b[128:]
            crosses.append(jnp.concatenate([ar * br + ai * bi, ar * bi - ai * br], 0))
        turns = [dot(inverse_ref[1 - second], cross) for cross in crosses]
        for k, i in enumerate(rows):
            turned = turns[k]
            extra = turned[:128, 128 * BLOCKS :]
            for b in range(BLOCKS):
                lanes = slice(128 * b, 128 * b + 128)
                moved = extra if b == 0 else pltpu.roll(extra, 128 - b, 1)
                imag = jnp.where(slot, moved, turned[128:, lanes]).astype(BF16)
                out = dot(jnp.concatenate([turned[:128, lanes].astype(BF16), imag], 1), last_ref[...])
                for w in range(2):
                    piece = out[:, 128 * w : 128 * w + 128]
                    j = 2 * b + w
                    surface[k, j, 8:136, :] = piece
                    surface[k, j, 0:8, :] = piece[120:]
                    surface[k, j, 136:144, :] = piece[:8]
                    peak_rows[j, pl.ds(i, 1), :] = jnp.max(jnp.abs(piece), axis=0, keepdims=True)
        for k, i in enumerate(rows):
            held = jnp.zeros((8, 128), F32)
            for j in range(2 * BLOCKS):
                dy = peaks[i, 0, j]
                dx = peaks[i, 1, j]
                piece = surface[k, j, pl.ds(dy + 6, 8), :]
                shift = lax.rem(8 * j + 2 + 128 - dx, 128)
                held = jnp.where(lane8 == j, pltpu.roll(piece, shift, 1), held)
            windows[i] = held

    def energy(sums):
        rows = jnp.concatenate([sums[0:10, :] + sums[1:11, :], jnp.zeros((6, LANES), F32)], 0)
        return exact_dot(rows, spread_ref[...])[0:10] / float(PATCH * PATCH)

    own_energy = energy(own_sums)
    other_rows(jnp.int32(0), STRIDE)

    def step(t, carry):
        start = pl.multiple_of(128 * t + 64, 64)
        rows = other.at[pl.ds(start, 128), main]

        pl.when(t == 1)(lambda: wait_for(LATER_EDGE))

        @pl.when(pair)
        def _():
            pltpu.make_async_remote_copy(
                src_ref=rows, dst_ref=rows, send_sem=send_sems.at[base + 1 + t], recv_sem=recv_sems.at[base + 1 + t],
                device_id=place.device((0, 0, 0)), device_id_type=pl.DeviceIdType.MESH,
            ).wait_recv()

        other_rows(start, 128)
        patch_rows((2 * t, 2 * t + 1))
        return carry

    lax.fori_loop(0, STEPS - 1, step, 0)
    wait_for(base + STEPS)
    wait_for(FORWARD)
    wait_for(CORNER)
    other_rows(jnp.int32(576), 128)
    scale = float(PATCH) ** 3 * jnp.sqrt((own_energy + 1e-05) * (energy(other_sums) + 1e-05))
    patch_rows((8, 9))

    group = lax.rem(lax.broadcasted_iota(jnp.int32, (10, 128), 1), 16)
    peak = jnp.zeros((10, 128), F32)
    for j in range(2 * BLOCKS):
        peak = jnp.where(group == j, jnp.max(peak_rows[j, 0:10, :], axis=1, keepdims=True), peak)
    height = peak / scale + 1e-05
    sums = jnp.concatenate([jnp.sum(windows[...] * basis_ref[e][None], axis=1) for e in range(6)], 0)
    values = exact_dot(sums, gather_ref[...])
    joined = values[0:16]
    for e in range(1, 6):
        joined = joined + pltpu.roll(values[16 * e : 16 * e + 16], 16 * e, 1)
    result[0:10, :] = joined[0:10] / scale / height
    send(RETURN)

    def give(coefficients):
        for e in range(6):
            moved = coefficients if e == 0 else pltpu.roll(coefficients, 128 - 16 * e, 1)
            out_ref[e, :, 0, :] = moved[0:10, :10] * valid[:, 0, :].astype(F32)

    for n in range(len(copies)):
        if n != RETURN:
            sent(n)

    @pl.when(jnp.logical_not(is_second))
    def _():
        give(result[...])

    @pl.when(is_second)
    def _():
        wait_for(RETURN)
        give(returned[...])

    sent(RETURN)


def correlate(tile, peaks, valid):
    tables = host_tables()
    apart = pl.BlockSpec(memory_space=pltpu.HBM)
    count = 9 + STEPS + 1
    return pl.pallas_call(
        kernel,
        out_shape=jax.ShapeDtypeStruct((6, 10, 1, 10), F32),
        in_specs=[apart] * (3 + len(tables)),
        out_specs=pl.BlockSpec(memory_space=pltpu.VMEM),
        scratch_shapes=[
            pltpu.VMEM((ROWS, LANES), BF16),
            pltpu.VMEM((ROWS, LANES), BF16),
            pltpu.VMEM((MAIN // 2, 128), BF16),
            pltpu.VMEM((ROWS // 2, 128), BF16),
            pltpu.VMEM((ROWS // 2, 128), BF16),
            *[pltpu.VMEM(t.shape, t.dtype) for t in tables],
            pltpu.VMEM((ROWS, LANES), BF16),
            pltpu.VMEM((ROWS, LANES), BF16),
            pltpu.VMEM((ROWS, LANES), BF16),
            pltpu.VMEM((ROWS, LANES), BF16),
            pltpu.VMEM((10, 256, LANES), BF16),
            pltpu.VMEM((16, LANES), F32),
            pltpu.VMEM((16, LANES), F32),
            pltpu.VMEM((2, 10, 144, 128), F32),
            pltpu.VMEM((16, 8, 128), F32),
            pltpu.VMEM((10, 16, 128), F32),
            pltpu.VMEM((16, 128), F32),
            pltpu.VMEM((16, 128), F32),
            pltpu.VMEM((10, 2, 10), jnp.int32),
            pltpu.VMEM((10, 1, 10), jnp.int32),
            pltpu.SMEM((10, 2, 10), jnp.int32),
            pltpu.SemaphoreType.DMA((3 + len(tables),)),
            pltpu.SemaphoreType.DMA((count,)),
            pltpu.SemaphoreType.DMA((count,)),
        ],
        compiler_params=pltpu.CompilerParams(
            collective_id=0, has_side_effects=True, vmem_limit_bytes=62 * 1024 * 1024
        ),
    )(tile, peaks, valid, *[jnp.asarray(t) for t in tables])


def body(sections, peaks, valid):
    out = correlate(sections[0], jnp.transpose(peaks, (0, 2, 1, 3))[0], jnp.transpose(valid, (1, 0, 2)))
    return jnp.transpose(out, (2, 0, 1, 3))


def solution(mesh):
    in_specs = (P("gz", "gy", "gx"), P("gz", None, "gy", "gx"), P("gz", "gy", "gx"))
    out_specs = P("gz", None, "gy", "gx")
    return jax.shard_map(body, mesh=mesh, in_specs=in_specs, out_specs=out_specs, check_vma=False)
```

```python
import functools
import math

import jax
import jax.numpy as jnp
import ml_dtypes
import numpy as np
from jax import lax
from jax.experimental import pallas as pl
from jax.experimental.pallas import tpu as pltpu
from jax.sharding import PartitionSpec as P

PATCH = 128
STRIDE = 64
WIN = 5
HALF = 64
ROWS = 704
LANES = 768
BLOCKS = 5
STEPS = 5
F32 = jnp.float32
BF16 = jnp.bfloat16


def host_tables():
    index = np.arange(PATCH)
    phase = ((index[:, None] * index[None, :]) % PATCH).astype(np.float32) * np.float32(
        2.0 * math.pi / PATCH
    )
    rounded = lambda v: v.astype(ml_dtypes.bfloat16).astype(np.float32)
    cosine, sine = rounded(np.cos(phase)), rounded(np.sin(phase))
    first = np.zeros((256, 256), np.float32)
    last = np.zeros((256, 256), np.float32)
    weight = np.where(np.arange(HALF) == 0, 1.0, 2.0).astype(np.float32)
    for w in range(2):
        rows = slice(64 * w, 64 * w + 128)
        real, imag = slice(64 * w, 64 * w + 64), slice(128 + 64 * w, 192 + 64 * w)
        lags = slice(128 * w, 128 * w + 128)
        first[rows, real] = cosine[:HALF].T
        first[rows, imag] = -sine[:HALF].T
        first[rows, 128 + 64 * w] = 0.0
        last[real, lags] = (cosine[:, :HALF] * weight).T
        last[imag, lags] = (-sine[:, :HALF] * weight).T
        last[128 + 64 * w, lags] = cosine[:, HALF]
    nyquist = np.zeros((LANES, 128), np.float32)
    for b in range(BLOCKS):
        for w in range(2):
            start = 128 * b + 64 * w
            nyquist[start : start + 128, b + 64 * w] = cosine[HALF]
    forward = np.block([[cosine, sine], [-sine, cosine]])
    inverse = np.stack([np.block([[cosine, sine], [sine, -cosine]]), np.block([[cosine, -sine], [sine, cosine]])])
    offsets = np.arange(WIN, dtype=np.float32) - WIN // 2
    ones = np.ones(WIN, np.float32)
    square = offsets * offsets - np.mean(offsets * offsets)
    pairs = [(ones, ones), (offsets, ones), (ones, offsets), (square, ones), (ones, square), (offsets, offsets)]
    basis = np.zeros((6, 8, 128), np.float32)
    for e, (p, q) in enumerate(pairs):
        func = p[:, None] * q[None, :]
        func = func / np.sqrt(np.sum(func * func))
        for j in range(2 * BLOCKS):
            basis[e, :WIN, 8 * j : 8 * j + WIN] = func
    gather = np.zeros((128, 128), np.float32)
    for j in range(2 * BLOCKS):
        gather[8 * j : 8 * j + 8, j] = 1.0
    spread = np.zeros((LANES, 128), np.float32)
    for j in range(2 * BLOCKS):
        for e in range(6):
            spread[64 * j : 64 * j + 128, 16 * e + j] = 1.0
    low = lambda v: v.astype(ml_dtypes.bfloat16)
    return low(first), low(nyquist), low(forward), low(inverse), low(last), basis, low(gather), low(spread)


def dot(a, b, precision=None):
    return lax.dot_general(a, b, (((1,), (0,)), ((), ())), precision=precision, preferred_element_type=F32)


def exact_dot(x, table):
    high = x.astype(BF16)
    rest = x - high.astype(F32)
    middle = rest.astype(BF16)
    low = (rest - middle.astype(F32)).astype(BF16)
    count = x.shape[0]
    out = dot(jnp.concatenate([high, middle, low], 0), table)
    return out[:count] + out[count : 2 * count] + out[2 * count :]


def row_transform(x, first_ref, block):
    return dot(x[:, 128 * block : 128 * block + 256], first_ref[...]).astype(BF16)


def unpack(packed):
    wide = packed.astype(F32)
    return jnp.concatenate([wide, pltpu.roll(wide, HALF, 1)], 0).astype(BF16)


def square_sums(x, sums_ref, strip):
    x = x.astype(F32)
    sums_ref[pl.ds(strip, 1), :] = jnp.sum(x * x, axis=0, keepdims=True)


def column_transform(real_ref, imag_ref, start, forward_ref, lanes=slice(0, LANES)):
    data = jnp.concatenate([real_ref[pl.ds(start, 128), lanes], imag_ref[pl.ds(start, 128), lanes]], 0)
    return dot(forward_ref[...], data).astype(BF16)


MAIN = 640


class Place:
    def __init__(self):
        self.at = {name: lax.axis_index(name) for name in ("gz", "gx", "gy")}
        self.size = {name: lax.axis_size(name) for name in ("gz", "gx", "gy")}

    def there(self, step):
        inside = None
        for name, move in zip(("gz", "gx", "gy"), step):
            if not (isinstance(move, int) and move == 0):
                to = self.at[name] + move
                ok = jnp.logical_and(to >= 0, to < self.size[name])
                inside = ok if inside is None else jnp.logical_and(inside, ok)
        return inside

    def device(self, step):
        return {name: self.at[name] + move for name, move in zip(("gz", "gx", "gy"), step)}


def kernel(tile_ref, peaks_ref, valid_hbm, first_hbm, nyquist_hbm, forward_hbm, inverse_hbm, last_hbm, basis_hbm, gather_hbm,
           spread_hbm, out_ref,
           own, other, packed, own_edge, other_edge,
           first_ref, nyquist_ref, forward_ref, inverse_ref, last_ref, basis_ref, gather_ref, spread_ref,
           own_re, own_im, other_re, other_im, spectra, own_sums, other_sums, surface, windows, peak_rows,
           result, returned, far_peaks, valid, peaks, local_sems, send_sems, recv_sems):
    place = Place()
    second = 1 - lax.rem(place.at["gx"], 2)
    is_second = second == 1
    ahead = 2 * second - 1
    tables = [(first_hbm, first_ref), (nyquist_hbm, nyquist_ref), (forward_hbm, forward_ref), (inverse_hbm, inverse_ref),
              (last_hbm, last_ref), (basis_hbm, basis_ref), (gather_hbm, gather_ref), (spread_hbm, spread_ref)]
    main = pl.ds(0, MAIN)
    tile_copy = pltpu.make_async_copy(tile_ref, own.at[main, main], local_sems.at[0])
    local_peaks = pltpu.make_async_copy(peaks_ref, peaks, local_sems.at[1])
    tables.append((valid_hbm, valid))
    local = [pltpu.make_async_copy(a, b, local_sems.at[2 + n]) for n, (a, b) in enumerate(tables)]

    pair = place.there((-ahead, 0, 0))
    beside = place.there((0, 1, 0))
    top = pl.ds(0, STRIDE)
    low = pl.ds(MAIN, STRIDE)
    first32, last32 = pl.ds(0, 32), pl.ds(MAIN // 2, 32)
    copies = [
        ((0, 0, -1), (0, 0, 1), tile_ref.at[top, :], own.at[low, main], None),
        ((0, -1, 0), (0, 1, 0), packed, own_edge.at[pl.ds(0, MAIN // 2)], None),
        ((0, 0, -1), (0, 0, 1), own_edge.at[first32], own_edge.at[last32], beside),
        ((ahead, 0, 0), (-ahead, 0, 0), peaks_ref, far_peaks, is_second),
        ((-ahead, 0, 0), (ahead, 0, 0), result, returned, is_second),
        ((-ahead, -1, 0), (-ahead, 1, 0), packed.at[pl.ds(0, 96)], other_edge.at[pl.ds(0, 96)], None),
        ((-ahead, -1, 0), (-ahead, 1, 0), packed.at[pl.ds(96, 224)], other_edge.at[pl.ds(96, 224)], None),
        ((0, 0, -1), (0, 0, 1), other_edge.at[first32], other_edge.at[last32], jnp.logical_and(pair, beside)),
        ((0, 0, -1), (0, 0, 1), other.at[top, main], other.at[low, main], pair),
    ]
    FAR, RETURN, EDGE, LATER_EDGE, CORNER, FORWARD = 3, 4, 5, 6, 7, 8
    base = len(copies)
    for start, count in [(0, 64)] + [(64 + 128 * t, 128) for t in range(STEPS - 1)] + [(576, 64)]:
        rows = pl.ds(start, count)
        copies.append(((ahead, 0, 0), (-ahead, 0, 0), tile_ref.at[rows, :], other.at[rows, main], None))

    def remote(n):
        step, _, source, destination, _ = copies[n]
        return pltpu.make_async_remote_copy(
            src_ref=source, dst_ref=destination, send_sem=send_sems.at[n], recv_sem=recv_sems.at[n],
            device_id=place.device(step), device_id_type=pl.DeviceIdType.MESH,
        )

    def when(n, side):
        ok = place.there(copies[n][side])
        return ok if copies[n][4] is None else jnp.logical_and(ok, copies[n][4])

    def send(n):
        pl.when(when(n, 0))(lambda: remote(n).start())

    def sent(n):
        pl.when(when(n, 0))(lambda: remote(n).wait_send())

    def wait_for(n):
        pl.when(when(n, 1))(lambda: remote(n).wait_recv())

    @pl.when(place.at["gy"] == place.size["gy"] - 1)
    def _():
        own[MAIN:ROWS, :MAIN] = jnp.zeros((STRIDE, MAIN), BF16)
        own_edge[MAIN // 2 :, :] = jnp.zeros((32, 128), BF16)
        other[MAIN:ROWS, :MAIN] = jnp.zeros((STRIDE, MAIN), BF16)
        other_edge[MAIN // 2 :, :] = jnp.zeros((32, 128), BF16)

    @pl.when(place.at["gx"] == place.size["gx"] - 1)
    def _():
        own_edge[...] = jnp.zeros_like(own_edge)
        other_edge[...] = jnp.zeros_like(other_edge)

    @pl.when(jnp.logical_not(pair))
    def _():
        other[:, :MAIN] = jnp.zeros((ROWS, MAIN), BF16)
        other_edge[...] = jnp.zeros_like(other_edge)
        far_peaks[...] = jnp.zeros_like(far_peaks)

    @pl.when(place.at["gz"] == place.size["gz"] - 1)
    def _():
        returned[...] = jnp.zeros_like(returned)

    barrier = pltpu.get_barrier_semaphore()
    meetings = [((0, 0, -1), (0, 0, 1)), ((0, -1, 0), (0, 1, 0)), ((ahead, 0, 0), (-ahead, 0, 0)),
                ((-ahead, 0, 0), (ahead, 0, 0)), ((-ahead, -1, 0), (-ahead, 1, 0))]
    for _, step in meetings:
        @pl.when(place.there(step))
        def _():
            pl.semaphore_signal(barrier, inc=1, device_id=place.device(step), device_id_type=pl.DeviceIdType.MESH)
    tile_copy.start()
    for copy in local:
        copy.start()
    pl.when(jnp.logical_not(is_second))(lambda: local_peaks.start())
    left = lax.broadcasted_iota(jnp.int32, (32, 128), 1) < HALF
    tile_copy.wait()
    for n in range(MAIN // STRIDE):
        block = own[STRIDE * n : STRIDE * n + STRIDE, 0:128].astype(F32)
        packed[32 * n : 32 * n + 32, :] = jnp.where(left, block[:32], pltpu.roll(block[32:], HALF, 1)).astype(BF16)
    pl.semaphore_wait(barrier, sum(place.there(step).astype(jnp.int32) for step, _ in meetings))
    for n in (1, EDGE, 0, base, FAR, LATER_EDGE, *range(base + 1, len(copies))):
        send(n)

    windows[...] = jnp.zeros_like(windows)
    peak_rows[...] = jnp.zeros_like(peak_rows)
    for copy in local:
        copy.wait()

    def keep(re, im, rows, b, out):
        re[rows, 128 * b : 128 * b + 128] = out[:, :128]
        im[rows, 128 * b : 128 * b + 128] = out[:, 128:]

    def keep_nyquist(re, im, rows, out):
        re[rows, 128 * BLOCKS :] = out
        im[rows, 128 * BLOCKS :] = jnp.zeros((out.shape[0], 128), BF16)

    for b in range(BLOCKS - 1):
        keep(own_re, own_im, slice(0, MAIN), b, row_transform(own[0:MAIN, :], first_ref, b))
    near, distant = is_second, jnp.logical_not(is_second)

    def pass_own_corner():
        wait_for(1)
        send(2)

    def pass_corner():
        wait_for(EDGE)
        send(CORNER)

    pl.when(near)(pass_own_corner)
    wait_for(base)
    send(FORWARD)
    pl.when(near)(pass_corner)
    wait_for(0)
    for b in range(BLOCKS - 1):
        keep(own_re, own_im, slice(MAIN, ROWS), b, row_transform(own[MAIN:ROWS, :], first_ref, b))

    def own_spectra(lanes, count):
        def some(i, carry):
            for k in range(count):
                row = count * i + k
                start = pl.multiple_of(row * STRIDE, STRIDE)
                spectra[row, :, lanes] = column_transform(own_re, own_im, start, forward_ref, lanes)
            return carry

        lax.fori_loop(0, 10 // count, some, 0)

    pl.when(distant)(lambda: own_spectra(slice(0, 512), 10))
    pl.when(distant)(pass_own_corner)
    pl.when(distant)(pass_corner)
    wait_for(2)

    def own_strip(strip, carry):
        rows = pl.ds(pl.multiple_of(strip * STRIDE, STRIDE), STRIDE)
        own[rows, MAIN:] = unpack(own_edge[pl.ds(pl.multiple_of(strip * 32, 32), 32), :])
        square_sums(own[rows, :], own_sums, strip)
        return carry

    lax.fori_loop(0, ROWS // STRIDE, own_strip, 0, unroll=True)
    keep(own_re, own_im, slice(0, ROWS), BLOCKS - 1, row_transform(own[...], first_ref, BLOCKS - 1))
    keep_nyquist(own_re, own_im, slice(0, ROWS), dot(own[...], nyquist_ref[...]).astype(BF16))
    wait_for(FAR)
    far = pltpu.make_async_copy(far_peaks, peaks, local_sems.at[1])
    pl.when(is_second)(lambda: far.start())
    pl.when(near)(lambda: own_spectra(slice(0, LANES), 10))
    pl.when(distant)(lambda: own_spectra(slice(512, LANES), 10))
    pl.when(is_second)(lambda: far.wait())
    pl.when(jnp.logical_not(is_second))(lambda: local_peaks.wait())

    lane = lax.broadcasted_iota(jnp.int32, (128, 128), 1)
    slot = lax.rem(lane, HALF) == 0
    lane8 = lax.broadcasted_iota(jnp.int32, (8, 128), 1) // 8

    def other_rows(start, count):
        rows = pl.ds(pl.multiple_of(start, STRIDE), count)
        for k in range(count // STRIDE):
            strip = lax.div(start, STRIDE) + k
            here = pl.ds(pl.multiple_of(strip * STRIDE, STRIDE), STRIDE)
            edge = unpack(other_edge[pl.ds(pl.multiple_of(strip * 32, 32), 32), :])
            other[here, MAIN:] = edge
            square_sums(jnp.concatenate([other[here, :MAIN], edge], 1), other_sums, strip)
        x = other[rows, :]
        for b in range(BLOCKS):
            keep(other_re, other_im, rows, b, row_transform(x, first_ref, b))
        keep_nyquist(other_re, other_im, rows, dot(x, nyquist_ref[...]).astype(BF16))

    def patch_rows(rows):
        crosses = []
        theirs = [column_transform(other_re, other_im, pl.multiple_of(i * STRIDE, STRIDE), forward_ref) for i in rows]
        for i, b in zip(rows, theirs):
            a = spectra[i]
            ar, ai, br, bi = a[:128], a[128:], b[:128], b[128:]
            crosses.append(jnp.concatenate([ar * br + ai * bi, ar * bi - ai * br], 0))
        turns = [dot(inverse_ref[1 - second], cross) for cross in crosses]
        for k, i in enumerate(rows):
            turned = turns[k]
            extra = turned[:128, 128 * BLOCKS :]
            for b in range(BLOCKS):
                lanes = slice(128 * b, 128 * b + 128)
                moved = extra if b == 0 else pltpu.roll(extra, 128 - b, 1)
                imag = jnp.where(slot, moved, turned[128:, lanes]).astype(BF16)
                out = dot(jnp.concatenate([turned[:128, lanes].astype(BF16), imag], 1), last_ref[...])
                for w in range(2):
                    piece = out[:, 128 * w : 128 * w + 128]
                    j = 2 * b + w
                    surface[k, j, 8:136, :] = piece
                    surface[k, j, 0:8, :] = piece[120:]
                    surface[k, j, 136:144, :] = piece[:8]
                    peak_rows[j, pl.ds(i, 1), :] = jnp.max(jnp.abs(piece), axis=0, keepdims=True)
        for k, i in enumerate(rows):
            held = jnp.zeros((8, 128), F32)
            for j in range(2 * BLOCKS):
                dy = peaks[i, 0, j]
                dx = peaks[i, 1, j]
                piece = surface[k, j, pl.ds(dy + 6, 8), :]
                shift = lax.rem(8 * j + 2 + 128 - dx, 128)
                held = jnp.where(lane8 == j, pltpu.roll(piece, shift, 1), held)
            windows[i] = held

    def energy(sums):
        rows = jnp.concatenate([sums[0:10, :] + sums[1:11, :], jnp.zeros((6, LANES), F32)], 0)
        return exact_dot(rows, spread_ref[...])[0:10] / float(PATCH * PATCH)

    own_energy = energy(own_sums)
    other_rows(jnp.int32(0), STRIDE)

    def step(t, carry):
        start = pl.multiple_of(128 * t + 64, 64)
        rows = other.at[pl.ds(start, 128), main]

        pl.when(t == 1)(lambda: wait_for(LATER_EDGE))

        @pl.when(pair)
        def _():
            pltpu.make_async_remote_copy(
                src_ref=rows, dst_ref=rows, send_sem=send_sems.at[base + 1 + t], recv_sem=recv_sems.at[base + 1 + t],
                device_id=place.device((0, 0, 0)), device_id_type=pl.DeviceIdType.MESH,
            ).wait_recv()

        other_rows(start, 128)
        patch_rows((2 * t, 2 * t + 1))
        return carry

    for t in range(STEPS - 1):
        step(jnp.int32(t), 0)
    wait_for(base + STEPS)
    wait_for(FORWARD)
    wait_for(CORNER)
    other_rows(jnp.int32(576), 128)
    scale = float(PATCH) ** 3 * jnp.sqrt((own_energy + 1e-05) * (energy(other_sums) + 1e-05))
    patch_rows((8, 9))

    group = lax.rem(lax.broadcasted_iota(jnp.int32, (10, 128), 1), 16)
    peak = jnp.zeros((10, 128), F32)
    for j in range(2 * BLOCKS):
        peak = jnp.where(group == j, jnp.max(peak_rows[j, 0:10, :], axis=1, keepdims=True), peak)
    height = peak / scale + 1e-05
    sums = jnp.concatenate([jnp.sum(windows[...] * basis_ref[e][None], axis=1) for e in range(6)], 0)
    values = exact_dot(sums, gather_ref[...])
    joined = values[0:16]
    for e in range(1, 6):
        joined = joined + pltpu.roll(values[16 * e : 16 * e + 16], 16 * e, 1)
    result[0:10, :] = joined[0:10] / scale / height
    send(RETURN)

    def give(coefficients):
        for e in range(6):
            moved = coefficients if e == 0 else pltpu.roll(coefficients, 128 - 16 * e, 1)
            out_ref[e, :, 0, :] = moved[0:10, :10] * valid[:, 0, :].astype(F32)

    for n in range(len(copies)):
        if n != RETURN:
            sent(n)

    @pl.when(jnp.logical_not(is_second))
    def _():
        give(result[...])

    @pl.when(is_second)
    def _():
        wait_for(RETURN)
        give(returned[...])

    sent(RETURN)


def correlate(tile, peaks, valid):
    tables = host_tables()
    apart = pl.BlockSpec(memory_space=pltpu.HBM)
    count = 9 + STEPS + 1
    return pl.pallas_call(
        kernel,
        out_shape=jax.ShapeDtypeStruct((6, 10, 1, 10), F32),
        in_specs=[apart] * (3 + len(tables)),
        out_specs=pl.BlockSpec(memory_space=pltpu.VMEM),
        scratch_shapes=[
            pltpu.VMEM((ROWS, LANES), BF16),
            pltpu.VMEM((ROWS, LANES), BF16),
            pltpu.VMEM((MAIN // 2, 128), BF16),
            pltpu.VMEM((ROWS // 2, 128), BF16),
            pltpu.VMEM((ROWS // 2, 128), BF16),
            *[pltpu.VMEM(t.shape, t.dtype) for t in tables],
            pltpu.VMEM((ROWS, LANES), BF16),
            pltpu.VMEM((ROWS, LANES), BF16),
            pltpu.VMEM((ROWS, LANES), BF16),
            pltpu.VMEM((ROWS, LANES), BF16),
            pltpu.VMEM((10, 256, LANES), BF16),
            pltpu.VMEM((16, LANES), F32),
            pltpu.VMEM((16, LANES), F32),
            pltpu.VMEM((2, 10, 144, 128), F32),
            pltpu.VMEM((16, 8, 128), F32),
            pltpu.VMEM((10, 16, 128), F32),
            pltpu.VMEM((16, 128), F32),
            pltpu.VMEM((16, 128), F32),
            pltpu.VMEM((10, 2, 10), jnp.int32),
            pltpu.VMEM((10, 1, 10), jnp.int32),
            pltpu.SMEM((10, 2, 10), jnp.int32),
            pltpu.SemaphoreType.DMA((3 + len(tables),)),
            pltpu.SemaphoreType.DMA((count,)),
            pltpu.SemaphoreType.DMA((count,)),
        ],
        compiler_params=pltpu.CompilerParams(
            collective_id=0, has_side_effects=True, vmem_limit_bytes=62 * 1024 * 1024
        ),
    )(tile, peaks, valid, *[jnp.asarray(t) for t in tables])


def body(sections, peaks, valid):
    out = correlate(sections[0], jnp.transpose(peaks, (0, 2, 1, 3))[0], jnp.transpose(valid, (1, 0, 2)))
    return jnp.transpose(out, (2, 0, 1, 3))


def solution(mesh):
    in_specs = (P("gz", "gy", "gx"), P("gz", None, "gy", "gx"), P("gz", "gy", "gx"))
    out_specs = P("gz", None, "gy", "gx")
    return jax.shard_map(body, mesh=mesh, in_specs=in_specs, out_specs=out_specs, check_vma=False)
```
